128 devices in a mesh: dp: 16 (over z, x), seq: 8 (over y, core).
Axes of the slice: x: 4, y: 4, z: 4, core: 2. Of those that a mesh axis runs over, the one named last changes fastest.
Arguments:
- queries: bfloat16 [16384, 4096], P(('dp', 'seq')), may hold values from -6 to 6
- keys: bfloat16 [16384, 4096], P(('dp', 'seq')), may hold values from -6 to 6
- values: bfloat16 [16384, 4096], P(('dp', 'seq')), may hold values from -6 to 6
- grad_mixed: bfloat16 [16384, 4096], P(('dp', 'seq')), may hold values from -6 to 6
- doc_lengths: int32 [16, 8], replicated, may hold values from 1 to 512, 1024 in all within a row
- owner: int32 [16], replicated, may hold values from 0 to 15, each once
Outputs:
- mixed: bfloat16 [16384, 4096], P(('dp', 'seq'))
- grad_queries: bfloat16 [16384, 4096], P(('dp', 'seq'))
- grad_keys: bfloat16 [16384, 4096], P(('dp', 'seq'))
- grad_values: bfloat16 [16384, 4096], P(('dp', 'seq'))
The draws below stay inside these ranges and needn't reach their ends.
Inputs may be any that keep to these rules, and one draw needn't show every extreme that they name: `doc_lengths`: each row holds positive lengths that sum to 1024, the largest exactly 512. `owner`: a permutation of the data groups.
All inputs are finite; a program needn't handle non-finite values.
Results may differ from the reference program's by a relative error of at most 0.012.
Values may be sent and summed in bfloat16 or wider, within the bound.
No kernel may reach another device: no remote copies, remote signals or barrier semaphores. Data moves between devices by JAX's collectives and lax.ppermute only.
A program may use at most 128 MiB of HBM per device.

```python
import math
import jax
import jax.numpy as jnp
import numpy as np
from jax import lax

HEAD_TOTAL = 32
HEAD_DIM = 128
DOCS = 8
SEQUENCE_LENGTH = 1024
TOKEN_TOTAL = 16384
N_DP = 16


def head_law(key, lowest, highest):
    rate_key = jax.random.fold_in(key, 101)
    sign_key = jax.random.fold_in(key, 102)
    spans = jnp.exp(jax.random.uniform(rate_key, (HEAD_TOTAL,), jnp.float32, math.log(lowest), math.log(highest)))
    middle_point = jnp.minimum(jnp.log(spans / (SEQUENCE_LENGTH // 2)) - 1.1, -1.0)
    direction = jnp.where(jax.random.bernoulli(sign_key, 0.5, (HEAD_TOTAL, HEAD_DIM)), 1.0, -1.0).astype(jnp.float32)
    return (middle_point, direction)


def draw_queries(key, part):
    highest = 12.0
    middle_point, direction = head_law(key, 0.2, highest)
    key = jax.random.fold_in(key, 1)
    jitter = jnp.clip(jax.random.normal(key, (TOKEN_TOTAL, HEAD_TOTAL, HEAD_DIM), jnp.float32), -4.0, 4.0)
    strength = -middle_point / math.sqrt(HEAD_DIM)
    result = strength[None, :, None] * direction[None] + jitter
    return result.reshape(TOKEN_TOTAL, HEAD_TOTAL * HEAD_DIM).astype(jnp.bfloat16)


def draw_keys(key, part):
    highest = 12.0
    middle_point, direction = head_law(key, 0.2, highest)
    key = jax.random.fold_in(key, 2)
    flurry_random_key = jax.random.fold_in(key, 7)
    jitter_key = jax.random.fold_in(key, 8)
    jitter = jnp.clip(jax.random.normal(jitter_key, (TOKEN_TOTAL, HEAD_TOTAL, HEAD_DIM), jnp.float32), -4.0, 4.0)
    token_flurries = jax.random.bernoulli(flurry_random_key, 2.0 / SEQUENCE_LENGTH, (TOKEN_TOTAL, HEAD_TOTAL))
    multiplier = jnp.where(token_flurries, 1.0 / middle_point[None, :], -1.0)
    result = multiplier[:, :, None] * direction[None] + jitter
    return result.reshape(TOKEN_TOTAL, HEAD_TOTAL * HEAD_DIM).astype(jnp.bfloat16)


def draw_values(key, part):
    key = jax.random.fold_in(key, 3)
    lean_key = jax.random.fold_in(key, 11)
    jitter_key = jax.random.fold_in(key, 12)
    column_lean = jax.random.uniform(lean_key, (HEAD_TOTAL * HEAD_DIM,), jnp.float32, -1.5, 1.5)
    jitter = jnp.clip(jax.random.normal(jitter_key, (TOKEN_TOTAL, HEAD_TOTAL * HEAD_DIM), jnp.float32), -4.0, 4.0)
    return (jitter + column_lean[None, :]).astype(jnp.bfloat16)


def draw_grad_mixed(key, part):
    key = jax.random.fold_in(key, 4)
    lean_key = jax.random.fold_in(key, 13)
    jitter_key = jax.random.fold_in(key, 14)
    column_lean = jax.random.uniform(lean_key, (HEAD_TOTAL * HEAD_DIM,), jnp.float32, -1.5, 1.5)
    jitter = jnp.clip(jax.random.normal(jitter_key, (TOKEN_TOTAL, HEAD_TOTAL * HEAD_DIM), jnp.float32), -4.0, 4.0)
    return (jitter + column_lean[None, :]).astype(jnp.bfloat16)


def split_up(amount, total, reach, lean):
    weights = [(1 << 20) // math.isqrt(standing ** lean) + 1 for standing in range(2, amount + 1)]
    spare, given = total - reach - (amount - 1), [1] * (amount - 1)
    while spare > 0:
        candidates = [i for i in range(amount - 1) if given[i] < reach]
        mass, left = sum([weights[i] for i in candidates]), spare
        for i in candidates:
            addition = min(reach - given[i], max(1, left * weights[i] // mass), spare)
            given[i] = given[i] + addition
            spare = spare - addition
    return np.array([reach] + given)


def uneven_parts(own_key, amount, total, reach, skew):
    if amount == 2:
        one = jax.random.randint(own_key, (), max(1, total - reach), min(reach, total - 1) + 1)
        return jnp.stack([one, total - one])
    sizes = jnp.asarray(split_up(amount, total, reach, skew), jnp.int32)
    twos = (amount - 1) // 2
    donor, receiver = sizes[1:1 + 2 * twos:2], sizes[2:2 + 2 * twos:2]
    slack = jnp.minimum(donor - 1, reach - receiver)
    passed = jax.random.randint(jax.random.fold_in(own_key, 1), (twos,), 0, 1 << 20) % (slack + 1)
    sizes = sizes.at[1:1 + 2 * twos:2].set(donor - passed).at[2:2 + 2 * twos:2].set(receiver + passed)
    return sizes[jax.random.permutation(jax.random.fold_in(own_key, 2), amount)]


def setup_inputs(seed: int = 0) -> dict:
    splits = jax.random.split(jax.random.key(seed), 7)
    return {
        "queries": draw_queries(jax.random.fold_in(splits[6], 71), 0),
        "keys": draw_keys(jax.random.fold_in(splits[6], 71), 0),
        "values": draw_values(jax.random.fold_in(splits[6], 71), 0),
        "grad_mixed": draw_grad_mixed(jax.random.fold_in(splits[6], 71), 0),
        "doc_lengths": jax.vmap(lambda own: uneven_parts(own, DOCS, SEQUENCE_LENGTH, SEQUENCE_LENGTH // 2, 2))(jax.random.split(splits[4], N_DP)).reshape((N_DP, DOCS)).astype(jnp.int32),
        "owner": jax.random.permutation(splits[5], N_DP).astype(jnp.int32),
    }


def doc_ids(lengths, count):
    ends = jnp.cumsum(lengths.astype(jnp.int32))
    places = jnp.arange(count, dtype=jnp.int32)
    return lax.optimization_barrier(jnp.sum((places[:, None] >= ends[None, :]).astype(jnp.int32), axis=1))

def head_grads(query, key_rows, value_rows, cotangent, doc):
    count = query.shape[0]
    places = jnp.arange(count, dtype=jnp.int32)
    allowed = (places[None, :] < places[:, None]) & (doc[:, None] == doc[None, :])
    scale = query.shape[1] ** (-0.5)

    def forward(qa, ka, va):
        scores = jnp.dot(qa, ka.T, preferred_element_type=jnp.float32) * scale
        spent = jnp.where(allowed, jax.nn.softplus(scores), 0.0)
        rest = lax.cumsum(spent, axis=1, reverse=True) - spent
        weight = jnp.where(allowed, jnp.exp(jax.nn.log_sigmoid(scores) - rest), 0.0)
        return jnp.dot(weight.astype(jnp.bfloat16), va, preferred_element_type=jnp.float32)
    out, pull = jax.vjp(forward, query, key_rows, value_rows)
    grad_q, grad_k, grad_v = pull(cotangent.astype(jnp.float32))
    return (out.astype(jnp.bfloat16), grad_q.astype(jnp.bfloat16), grad_k.astype(jnp.bfloat16), grad_v.astype(jnp.bfloat16))

def reference(queries, keys, values, grad_mixed, doc_lengths, owner):

    def split(x):
        return jnp.transpose(x.reshape(N_DP, SEQUENCE_LENGTH, HEAD_TOTAL, HEAD_DIM), (0, 2, 1, 3))

    def batch(items):
        qb, kb, vb, gb, lengths = items
        doc = doc_ids(lengths, SEQUENCE_LENGTH)
        return lax.map(lambda t: head_grads(t[0], t[1], t[2], t[3], doc), (qb, kb, vb, gb))
    outs = lax.map(batch, (split(queries), split(keys), split(values), split(grad_mixed), doc_lengths))

    def join(x):
        return jnp.transpose(x, (0, 2, 1, 3)).reshape(N_DP, SEQUENCE_LENGTH, HEAD_TOTAL * HEAD_DIM)
    out, grad_q, grad_k, grad_v = [join(x) for x in outs]
    placed = jnp.zeros_like(out).at[owner].set(out)
    width = HEAD_TOTAL * HEAD_DIM
    return (placed.reshape(TOKEN_TOTAL, width), grad_q.reshape(TOKEN_TOTAL, width), grad_k.reshape(TOKEN_TOTAL, width), grad_v.reshape(TOKEN_TOTAL, width))
```

```python
import functools

import jax
import jax.numpy as jnp
from jax import lax
from jax.experimental import pallas as pl
from jax.experimental.pallas import tpu as pltpu
from jax.sharding import PartitionSpec as P

HEAD_DIM = 128
LOG2E = 1.4426950408889634
ROWS = 256
NT = (((1,), (1,)), ((), ()))
TN = (((0,), (0,)), ((), ()))


def attention_rows(units, r0, refs, start_ref, tri_ref, dk_acc, dv_acc, outs):
    q_ref, k_ref, v_ref, g_ref = refs
    out_ref, dq_ref = outs
    scale = HEAD_DIM ** (-0.5)
    width = units * 128
    c0 = pl.multiple_of(r0 + ROWS - width, 128)

    def load(ref, first, count):
        return ref[pl.ds(first // 128, count // 128), 0].reshape(count, HEAD_DIM)

    def store(ref, x):
        ref[pl.ds(r0 // 128, ROWS // 128), 0] = x.astype(jnp.bfloat16).reshape(
            ROWS // 128, 128, HEAD_DIM
        )

    q, g = load(q_ref, r0, ROWS), load(g_ref, r0, ROWS)
    k, v = load(k_ref, c0, width), load(v_ref, c0, width)
    start = start_ref[pl.ds(r0, ROWS), :1] - c0
    row = lax.broadcasted_iota(jnp.int32, (ROWS, 1), 0) + (r0 - c0)

    edges = list(range(width, 0, -ROWS)) + [0]
    chunks = [(edges[i + 1], edges[i]) for i in range(len(edges) - 1)]
    carry = jnp.zeros((ROWS, 1), jnp.float32)
    out = jnp.zeros((ROWS, HEAD_DIM), jnp.float32)
    kept = []
    for lo, hi in chunks:
        n = hi - lo
        t = lax.dot_general(q, k[lo:hi], NT, preferred_element_type=jnp.float32) * (scale * LOG2E)
        col = lax.broadcasted_iota(jnp.int32, (ROWS, n), 1) + lo
        t = jnp.where((col >= start) & (col < row), t, -1e30)
        tail = jnp.log2(1.0 + jnp.exp2(-jnp.abs(t)))
        z = jnp.maximum(t, 0.0) + tail
        ls = jnp.minimum(t, 0.0) - tail
        rest = jnp.dot(
            z.astype(jnp.bfloat16), tri_ref[0, :n, :n], preferred_element_type=jnp.float32
        ) + carry
        carry = rest[:, :1] + z[:, :1]
        w = jnp.exp2(ls - rest)
        wb = w.astype(jnp.bfloat16)
        out += jnp.dot(wb, v[lo:hi], preferred_element_type=jnp.float32)
        dv_acc[pl.ds(pl.multiple_of(c0 + lo, 128), n), :] += lax.dot_general(
            wb, g, TN, preferred_element_type=jnp.float32
        )
        dw = lax.dot_general(g, v[lo:hi], NT, preferred_element_type=jnp.float32)
        kept.append((w * dw, jnp.exp2(ls)))
    store(out_ref, out)

    carry = jnp.zeros((ROWS, 1), jnp.float32)
    dq = jnp.zeros((ROWS, HEAD_DIM), jnp.float32)
    for (lo, hi), (a, sig) in reversed(list(zip(chunks, kept))):
        n = hi - lo
        upto = jnp.dot(
            a.astype(jnp.bfloat16), tri_ref[1, :n, :n], preferred_element_type=jnp.float32
        ) + (a + carry)
        carry = upto[:, n - 1 :]
        ds = (a - sig * upto).astype(jnp.bfloat16)
        dq += jnp.dot(ds, k[lo:hi], preferred_element_type=jnp.float32)
        dk_acc[pl.ds(pl.multiple_of(c0 + lo, 128), n), :] += lax.dot_general(
            ds, q, TN, preferred_element_type=jnp.float32
        )
    store(dq_ref, dq * scale)


def attention_kernel(
    units_ref, q_ref, k_ref, v_ref, g_ref, start_ref,
    out_ref, dq_ref, dk_ref, dv_ref, tri_ref, dk_acc, dv_acc,
):
    @pl.when(pl.program_id(0) == 0)
    def _():
        a = lax.broadcasted_iota(jnp.int32, (ROWS, ROWS), 0)
        b = lax.broadcasted_iota(jnp.int32, (ROWS, ROWS), 1)
        tri_ref[0] = jnp.where(a > b, 1.0, 0.0).astype(jnp.bfloat16)
        tri_ref[1] = jnp.where(a < b, 1.0, 0.0).astype(jnp.bfloat16)

    dk_acc[...] = jnp.zeros_like(dk_acc)
    dv_acc[...] = jnp.zeros_like(dv_acc)

    @pl.loop(0, dk_acc.shape[0] // ROWS)
    def _(i):
        r0 = pl.multiple_of(i * ROWS, ROWS)
        units = units_ref[i]
        for n in range(2, 7):
            @pl.when(units == n)
            def _():
                attention_rows(
                    n, r0, (q_ref, k_ref, v_ref, g_ref), start_ref, tri_ref,
                    dk_acc, dv_acc, (out_ref, dq_ref),
                )

    shape = dk_ref.shape
    dk_ref[...] = (dk_acc[...] * HEAD_DIM ** (-0.5)).astype(jnp.bfloat16).reshape(shape)
    dv_ref[...] = dv_acc[...].astype(jnp.bfloat16).reshape(shape)


def attention(x, start, units):
    blocks, _, rows, width = x.shape
    heads = width // HEAD_DIM
    count = blocks * rows
    block = (blocks, 1, rows, HEAD_DIM)
    part = jax.ShapeDtypeStruct((blocks, 1, rows, width), jnp.bfloat16)
    outs = pl.pallas_call(
        attention_kernel,
        out_shape=[part] * 4,
        grid_spec=pltpu.PrefetchScalarGridSpec(
            num_scalar_prefetch=1,
            grid=(heads,),
            in_specs=[
                pl.BlockSpec(block, functools.partial(lambda a, h, u: (0, a, 0, h), a))
                for a in range(4)
            ]
            + [pl.BlockSpec((count, 128), lambda h, u: (0, 0))],
            out_specs=[pl.BlockSpec(block, lambda h, u: (0, 0, 0, h))] * 4,
            scratch_shapes=[
                pltpu.VMEM((2, ROWS, ROWS), jnp.bfloat16),
                pltpu.VMEM((count, HEAD_DIM), jnp.float32),
                pltpu.VMEM((count, HEAD_DIM), jnp.float32),
            ],
        ),
        compiler_params=pltpu.CompilerParams(vmem_limit_bytes=40 * 1024 * 1024),
        cost_estimate=pl.CostEstimate(
            flops=16 * heads * count * count * HEAD_DIM // 2,
            bytes_accessed=8 * count * width * 2,
            transcendentals=2 * heads * count * count,
        ),
    )(units, x, x, x, x, start)
    return outs


def document_starts(lengths, count):
    firsts = jnp.cumsum(lengths) - lengths
    places = jnp.arange(count, dtype=jnp.int32)
    start = jnp.max(jnp.where(firsts[None, :] <= places[:, None], firsts[None, :], 0), axis=1)
    head = start[::ROWS]
    units = (places[::ROWS] + ROWS) // 128 - head // 128
    return jnp.broadcast_to(start[:, None], (count, 128)), jnp.clip(units, 2, 6).astype(jnp.int32)


def local(queries, keys, values, grad_mixed, doc_lengths, owner):
    rows, width = queries.shape
    group = lax.axis_index("dp")
    groups = lax.axis_size("dp")
    peers = lax.axis_size("seq")
    piece = width // peers

    lengths = lax.dynamic_index_in_dim(doc_lengths, group, 0, keepdims=False)
    start, units = document_starts(lengths, rows * peers)

    x = jnp.stack([queries, keys, values, grad_mixed]).reshape(4, rows, peers, piece)
    x = lax.all_to_all(
        jnp.transpose(x, (2, 0, 1, 3)), "seq", split_axis=0, concat_axis=0, tiled=True
    )
    out, dq, dk, dv = attention(x, start, units)

    grads = jnp.concatenate([dq, dk, dv], axis=1)
    grads = lax.all_to_all(grads, "seq", split_axis=0, concat_axis=0, tiled=True)
    grads = jnp.transpose(grads, (1, 2, 0, 3)).reshape(3, rows, width)

    small = rows // groups
    spread = jnp.transpose(out.reshape(peers, groups, small, piece), (1, 0, 2, 3))
    spread = lax.all_to_all(
        spread.reshape(groups * peers, small, piece), ("dp", "seq"),
        split_axis=0, concat_axis=0, tiled=True,
    ).reshape(groups, peers, small, piece)
    sender = jnp.argsort(owner)
    slots = jnp.take(spread, sender, axis=0)
    landed = lax.all_to_all(slots, "dp", split_axis=0, concat_axis=0, tiled=True)
    mixed = jnp.transpose(landed, (0, 2, 1, 3)).reshape(rows, width)
    return (mixed, grads[0], grads[1], grads[2])


def solution(mesh):
    placed = P(("dp", "seq"), None)
    return jax.shard_map(
        local,
        mesh=mesh,
        in_specs=(placed,) * 4 + (P(), P()),
        out_specs=(placed,) * 4,
        check_vma=False,
    )
```

```python
import jax
import jax.numpy as jnp
from jax import lax
from jax.experimental import pallas as pl
from jax.experimental.pallas import tpu as pltpu
from jax.sharding import PartitionSpec as P

HEAD_DIM = 128
LOG2E = 1.4426950408889634
SCALE = HEAD_DIM ** (-0.5)
ROWS = 256
CHIPS, CORES = 4, 2
PEERS = CHIPS * CORES
CHUNKS = 2
HP = 2
WIDTH = HP * HEAD_DIM
BLOCKS = PEERS * 128 // ROWS
DOCS = 8
FIRSTS = 2 + BLOCKS
WINDOW = 6 * 128
KEPT = (BLOCKS, ROWS, WINDOW)
NT = (((1,), (1,)), ((), ()))
TN = (((0,), (0,)), ((), ()))
ANY = pl.BlockSpec(memory_space=pl.ANY)
MIB = 1024 * 1024
VMEM = 20 * MIB


def position():
    me = lax.axis_index("seq")
    return lax.div(me, CORES), lax.rem(me, CORES)


def chip(y, d):
    return lax.rem(y + d + CHIPS, CHIPS)


def column(y, c, k):
    return pl.multiple_of((y * CHUNKS + k) * CORES * WIDTH + c * WIDTH, WIDTH)


def turn(x, d):
    pairs = [(i, (i // CORES + d) % CHIPS * CORES + i % CORES) for i in range(PEERS)]
    return lax.ppermute(x, "seq", pairs)


def swap_cores(x):
    return lax.ppermute(x, "seq", [(i, i ^ 1) for i in range(PEERS)])


def turn_all(xs):
    got = {d: turn(xs[d], d) for d in (1, 3, 2)}
    return [xs[0], got[1], got[2], got[3]]


def run_all(copies):
    for x in copies:
        x.start()
    for x in copies:
        x.wait()


def run_two_stages(into_vmem, out_of):
    for x in into_vmem:
        x.start()
    for x, nexts in zip(into_vmem, out_of):
        x.wait()
        for z in nexts:
            z.start()
    for nexts in out_of:
        for z in nexts:
            z.wait()


def copy_kernel(plan, inputs, shapes, copies, vmem):
    n = len(inputs)

    def kernel(*refs):
        pairs = plan(refs[:n], refs[n:-1])
        assert len(pairs) == copies
        run_all([pltpu.make_async_copy(a, b, refs[-1].at[i]) for i, (a, b) in enumerate(pairs)])

    return pl.pallas_call(
        kernel,
        out_shape=[jax.ShapeDtypeStruct(x, jnp.bfloat16) for x in shapes],
        in_specs=[ANY] * n,
        out_specs=[pl.BlockSpec(memory_space=pltpu.VMEM)] * len(shapes),
        scratch_shapes=[pltpu.SemaphoreType.DMA((copies,))],
        compiler_params=pltpu.CompilerParams(vmem_limit_bytes=vmem),
        cost_estimate=pl.CostEstimate(flops=10**9, bytes_accessed=MIB, transcendentals=0),
    )(*inputs)


def pack_chips(arrays, k):
    n, rows = len(arrays), arrays[0].shape[0]

    def plan(ins, outs):
        y, _ = position()
        return [
            (ins[a].at[:, pl.ds(column(chip(y, d), 0, k), CORES * WIDTH)], outs[d].at[a])
            for d in (1, 3, 2, 0)
            for a in range(n)
        ]

    return copy_kernel(plan, arrays, [(n, rows, CORES * WIDTH)] * CHIPS, CHIPS * n, 62 * MIB)


def pack_other_core(arrays, slabs):
    rows = arrays[0].shape[0]

    def plan(ins, outs):
        y, c = position()
        return [
            (ins[a].at[:, pl.ds(column(chip(y, d), 1 - c, k), WIDTH)], outs[0].at[d, i])
            for d in range(CHIPS)
            for i, (a, k) in enumerate(slabs)
        ]

    shape = (CHIPS, len(slabs), rows, WIDTH)
    return copy_kernel(plan, arrays, [shape], CHIPS * len(slabs), 62 * MIB)[0]


def merge_columns(arrays, swapped, slabs, cut):
    rows = arrays[0].shape[0]
    n = len(slabs)

    def plan(ins, outs):
        y, c = position()
        pairs = []
        for d in (1, 3, 2, 0):
            for i, (a, k) in enumerate(slabs):
                src = ins[a].at[:, pl.ds(column(chip(y, d), c, k), WIDTH)]
                dst = outs[d].at[0, i] if i < cut else outs[CHIPS + d].at[0, i - cut]
                pairs.append((src, dst))
            pairs.append((ins[-1].at[d, :cut], outs[d].at[1]))
            pairs.append((ins[-1].at[d, cut:], outs[CHIPS + d].at[1]))
        return pairs

    shapes = [(CORES, cut, rows, WIDTH)] * CHIPS + [(CORES, n - cut, rows, WIDTH)] * CHIPS
    outs = copy_kernel(plan, list(arrays) + [swapped], shapes, CHIPS * (n + 2), 62 * MIB)
    return outs[:CHIPS], outs[CHIPS:]


def pick_other_core_columns(got):
    n, rows, _ = got[0].shape

    def plan(ins, outs):
        _, c = position()
        first = pl.multiple_of((1 - c) * WIDTH, WIDTH)
        return [(ins[d].at[:, :, pl.ds(first, WIDTH)], outs[0].at[d]) for d in range(CHIPS)]

    return copy_kernel(plan, got, [(CHIPS, n, rows, WIDTH)], CHIPS, 16 * MIB)[0]


def pick_other_core_rows(got):
    def plan(ins, outs):
        return [(ins[d].at[1], outs[0].at[d]) for d in range(CHIPS)]

    return copy_kernel(plan, got, [(CHIPS,) + got[0].shape[1:]], CHIPS, 16 * MIB)[0]


def merge_rows(own, swapped):
    def plan(ins, outs):
        return [
            (ins[core].at[d], outs[i].at[core]) for i, d in enumerate((1, 2, 3)) for core in (0, 1)
        ]

    return copy_kernel(plan, [own, swapped], [(CORES,) + own.shape[1:]] * 3, 6, 16 * MIB)


def unpack(own, sib, into, k):
    flat = list(own) + list(sib)
    arrays = []
    for x, _ in flat:
        if not any(x is z for z in arrays):
            arrays.append(x)
    where = [next(i for i, z in enumerate(arrays) if z is x) for x, _ in flat]
    n, rows, width = arrays[0].shape[-3:]
    olds = [] if into is None else list(into)
    order = [i * CHIPS + d for d in (0, 1, 3, 2) for i in range(CORES)]

    def kernel(*refs):
        ins = refs[: len(arrays)]
        outs = refs[len(arrays) + len(olds) : -3]
        held, arrive, leave = refs[-3:]
        y, c = position()
        into_vmem, out_of = [], []
        for i in order:
            core = 1 - c if i >= CHIPS else c
            col = column(chip(y, -(i % CHIPS)), core, k)
            src = ins[where[i]].at[flat[i][1]]
            into_vmem.append(pltpu.make_async_copy(src, held.at[i], arrive.at[i]))
            out_of.append([
                pltpu.make_async_copy(
                    held.at[i, a], outs[a].at[:, pl.ds(col, width)], leave.at[i * n + a]
                )
                for a in range(n)
            ])
        run_two_stages(into_vmem, out_of)

    return pl.pallas_call(
        kernel,
        out_shape=[jax.ShapeDtypeStruct((rows, PEERS * CHUNKS * WIDTH), jnp.bfloat16)] * n,
        in_specs=[ANY] * (len(arrays) + len(olds)),
        out_specs=[ANY] * n,
        scratch_shapes=[
            pltpu.VMEM((PEERS, n, rows, width), jnp.bfloat16),
            pltpu.SemaphoreType.DMA((PEERS,)),
            pltpu.SemaphoreType.DMA((PEERS * n,)),
        ],
        compiler_params=pltpu.CompilerParams(vmem_limit_bytes=16 * MIB),
        input_output_aliases={len(arrays) + a: a for a in range(len(olds))},
        cost_estimate=pl.CostEstimate(flops=3 * 10**9, bytes_accessed=MIB, transcendentals=0),
    )(*arrays, *olds)


def pick(parts, sender):
    groups = parts[0].shape[0]
    n = len(parts)

    def kernel(sender_ref, *refs):
        ins, out, (held, arrive, leave) = refs[:n], refs[n], refs[n + 1 :]
        into_vmem, out_of = [], []
        for g in range(groups):
            for k in range(n):
                i = g * n + k
                into_vmem.append(
                    pltpu.make_async_copy(ins[k].at[sender_ref[g]], held.at[i], arrive.at[i])
                )
                out_of.append([pltpu.make_async_copy(held.at[i], out.at[g, k], leave.at[i])])
        run_two_stages(into_vmem, out_of)

    return pl.pallas_call(
        kernel,
        out_shape=jax.ShapeDtypeStruct((groups, n) + parts[0].shape[1:], jnp.bfloat16),
        grid_spec=pltpu.PrefetchScalarGridSpec(
            num_scalar_prefetch=1,
            grid=(1,),
            in_specs=[pl.BlockSpec(memory_space=pl.ANY)] * n,
            out_specs=pl.BlockSpec(memory_space=pl.ANY),
            scratch_shapes=[
                pltpu.VMEM((groups * n,) + parts[0].shape[1:], jnp.bfloat16),
                pltpu.SemaphoreType.DMA((groups * n,)),
                pltpu.SemaphoreType.DMA((groups * n,)),
            ],
        ),
        compiler_params=pltpu.CompilerParams(vmem_limit_bytes=VMEM),
    )(sender, *parts)


def settle(landed):
    _, chunks, peers, small, lanes = landed.shape
    groups = 8
    heads = landed.shape[0] // groups
    x = landed.reshape(heads, groups, chunks, peers, small, lanes)
    half = groups // 2

    def kernel(x_ref, o_ref):
        for s in range(peers):
            for k in range(chunks):
                for h in range(heads):
                    chip_, core = divmod(s, CORES)
                    col = (((chip_ * chunks + k) * CORES + core) * heads + h) * lanes
                    o_ref[:, col : col + lanes] = x_ref[h, :, k, s].reshape(half * small, lanes)

    return pl.pallas_call(
        kernel,
        out_shape=jax.ShapeDtypeStruct((groups * small, peers * chunks * heads * lanes), jnp.bfloat16),
        grid=(2,),
        in_specs=[
            pl.BlockSpec((heads, half, chunks, peers, small, lanes), lambda i: (0, i, 0, 0, 0, 0))
        ],
        out_specs=pl.BlockSpec((half * small, peers * chunks * heads * lanes), lambda i: (i, 0)),
        compiler_params=pltpu.CompilerParams(vmem_limit_bytes=VMEM),
    )(x)


def triangle(after):
    a = lax.broadcasted_iota(jnp.int32, (ROWS, ROWS), 0)
    b = lax.broadcasted_iota(jnp.int32, (ROWS, ROWS), 1)
    return jnp.where((a > b) if after else (a < b), 1.0, 0.0).astype(jnp.bfloat16)


def key_chunks(units):
    edges = list(range(units * 128, 0, -ROWS)) + [0]
    return [(edges[i + 1], edges[i]) for i in range(len(edges) - 1)]


def gather_rows(pieces, scratch, scalars_ref):
    y, c = scalars_ref[0], scalars_ref[1]
    for i, ref in enumerate(pieces):
        p = chip(y, -(i % CHIPS)) * CORES + (1 - c if i >= CHIPS else c)
        x = ref[...]
        scratch[:, pl.ds(p, 1)] = x.reshape((scratch.shape[0], 1) + scratch.shape[2:])


def row_block(scalars_ref, body):
    i = pl.program_id(0)
    r0 = pl.multiple_of(i * ROWS, ROWS)
    for n in range(2, 7):
        @pl.when(scalars_ref[2 + i] == n)
        def _():
            body(n, r0)


def rows_of(ref, a, first, count, h):
    x = ref[a, pl.ds(first // 128, count // 128), :, h * HEAD_DIM : (h + 1) * HEAD_DIM]
    return x.reshape(count, HEAD_DIM)


def forward_kernel(scalars_ref, *refs):
    pieces, (out_ref, qkv_ref, w_ref, sig_ref, tri_ref) = refs[:PEERS], refs[PEERS:]
    heads = range(HP)

    @pl.when(pl.program_id(0) == 0)
    def _():
        tri_ref[...] = triangle(True)
        gather_rows(pieces, qkv_ref, scalars_ref)

    def body(units, r0):
        c0 = pl.multiple_of(r0 + ROWS - units * 128, 128)
        row = lax.broadcasted_iota(jnp.int32, (ROWS, 1), 0) + (r0 - c0)
        start = jnp.zeros((ROWS, 1), jnp.int32) - c0
        for d in range(DOCS):
            first = scalars_ref[FIRSTS + d] - c0
            start = jnp.where(row >= first, jnp.maximum(start, first), start)
        q = [rows_of(qkv_ref, 0, r0, ROWS, h) for h in heads]
        rest = [jnp.zeros((ROWS, 1), jnp.float32)] * HP
        out = [jnp.zeros((ROWS, HEAD_DIM), jnp.float32)] * HP
        for lo, hi in key_chunks(units):
            n = hi - lo
            col = lax.broadcasted_iota(jnp.int32, (ROWS, n), 1) + lo
            allowed = (col >= start) & (col < row)
            for h in heads:
                k = rows_of(qkv_ref, 1, c0 + lo, n, h)
                v = rows_of(qkv_ref, 2, c0 + lo, n, h)
                t = lax.dot_general(q[h], k, NT, preferred_element_type=jnp.float32)
                t = jnp.where(allowed, t * (SCALE * LOG2E), -1e30)
                tail = jnp.log2(1.0 + jnp.exp2(-jnp.abs(t)))
                z = jnp.maximum(t, 0.0) + tail
                ls = jnp.minimum(t, 0.0) - tail
                after = jnp.dot(
                    z.astype(jnp.bfloat16), tri_ref[:n, :n], preferred_element_type=jnp.float32
                ) + rest[h]
                rest[h] = after[:, :1] + z[:, :1]
                w = jnp.exp2(ls - after).astype(jnp.bfloat16)
                out[h] += jnp.dot(w, v, preferred_element_type=jnp.float32)
                w_ref[h, 0, :, lo:hi] = w
                sig_ref[h, 0, :, lo:hi] = jnp.exp2(ls).astype(jnp.bfloat16)
        for h in heads:
            x = out[h].astype(jnp.bfloat16)
            for r in range(ROWS // 128):
                for g in range(8):
                    at = r * 128 + g * 16
                    out_ref[h * 8 + g, pl.ds(r0 // 128 + r, 1)] = x[at : at + 16].reshape(
                        1, 16, HEAD_DIM
                    )

    row_block(scalars_ref, body)


def backward_kernel(scalars_ref, *refs):
    pieces, (qkv_ref, w_ref, sig_ref) = refs[:PEERS], refs[PEERS : PEERS + 3]
    outs = refs[PEERS + 3 : -5]
    tri_ref, g_ref, dq_ref, dk_acc, dv_acc = refs[-5:]
    heads = range(HP)

    @pl.when(pl.program_id(0) == 0)
    def _():
        tri_ref[...] = triangle(False)
        gather_rows(pieces, g_ref, scalars_ref)
        dk_acc[...] = jnp.zeros_like(dk_acc)
        dv_acc[...] = jnp.zeros_like(dv_acc)

    def body(units, r0):
        c0 = pl.multiple_of(r0 + ROWS - units * 128, 128)
        q = [rows_of(qkv_ref, 0, r0, ROWS, h) for h in heads]
        g = [rows_of(g_ref, 0, r0, ROWS, h) for h in heads]
        upto = [jnp.zeros((ROWS, 1), jnp.float32)] * HP
        dq = [jnp.zeros((ROWS, HEAD_DIM), jnp.float32)] * HP
        for lo, hi in reversed(key_chunks(units)):
            n = hi - lo
            here = pl.ds(pl.multiple_of(c0 + lo, 128), n)
            for h in heads:
                k = rows_of(qkv_ref, 1, c0 + lo, n, h)
                v = rows_of(qkv_ref, 2, c0 + lo, n, h)
                w = w_ref[h, 0, :, lo:hi]
                dv_acc[h, here] += lax.dot_general(
                    w, g[h], TN, preferred_element_type=jnp.float32
                )
                dw = lax.dot_general(g[h], v, NT, preferred_element_type=jnp.float32)
                a = w.astype(jnp.float32) * dw
                total = jnp.dot(
                    a.astype(jnp.bfloat16), tri_ref[:n, :n], preferred_element_type=jnp.float32
                ) + (a + upto[h])
                upto[h] = total[:, n - 1 :]
                ds = a - sig_ref[h, 0, :, lo:hi].astype(jnp.float32) * total
                ds = ds.astype(jnp.bfloat16)
                dq[h] += jnp.dot(ds, k, preferred_element_type=jnp.float32)
                dk_acc[h, here] += lax.dot_general(
                    ds, q[h], TN, preferred_element_type=jnp.float32
                )
        for h in heads:
            dq_ref[h, pl.ds(r0, ROWS)] = (dq[h] * SCALE).astype(jnp.bfloat16)

    row_block(scalars_ref, body)

    @pl.when(pl.program_id(0) == BLOCKS - 1)
    def _():
        y, c = scalars_ref[0], scalars_ref[1]
        for i in range(PEERS):
            d, sib = i % CHIPS, i // CHIPS
            ref = outs[d].at[sib] if len(outs) == CHIPS else outs[sib].at[d]
            p = chip(y, d) * CORES + (1 - c if sib else c)
            at = pl.ds(pl.multiple_of(p * 128, 128), 128)
            for h in heads:
                cols = slice(h * HEAD_DIM, (h + 1) * HEAD_DIM)
                ref[0, :, cols] = dq_ref[h, at]
                ref[1, :, cols] = (dk_acc[h, at] * SCALE).astype(jnp.bfloat16)
                ref[2, :, cols] = dv_acc[h, at].astype(jnp.bfloat16)


def cost(microseconds):
    return pl.CostEstimate(
        flops=int(microseconds * 1.1e9), bytes_accessed=MIB, transcendentals=0
    )


def whole(shape):
    return pl.BlockSpec(shape, lambda i, u: (0,) * len(shape))


def forward(pieces, scalars):
    kept = jax.ShapeDtypeStruct((HP,) + KEPT, jnp.bfloat16)
    kept_spec = pl.BlockSpec((HP, 1) + KEPT[1:], lambda i, u: (0, i, 0, 0))
    out, qkv = (HP * 8, PEERS, 16, HEAD_DIM), (3, PEERS, 128, WIDTH)
    return pl.pallas_call(
        forward_kernel,
        out_shape=[jax.ShapeDtypeStruct(x, jnp.bfloat16) for x in (out, qkv)] + [kept, kept],
        grid_spec=pltpu.PrefetchScalarGridSpec(
            num_scalar_prefetch=1,
            grid=(BLOCKS,),
            in_specs=[spec for _, spec in pieces],
            out_specs=[whole(out), whole(qkv), kept_spec, kept_spec],
            scratch_shapes=[pltpu.VMEM((ROWS, ROWS), jnp.bfloat16)],
        ),
        compiler_params=pltpu.CompilerParams(vmem_limit_bytes=VMEM),
        cost_estimate=cost(8),
    )(scalars, *[x for x, _ in pieces])


def backward(pieces, saved, scalars, by_chip):
    count = PEERS * 128
    kept_spec = pl.BlockSpec((HP, 1) + KEPT[1:], lambda i, u: (0, i, 0, 0))
    outs = [(CORES, 3, 128, WIDTH)] * CHIPS if by_chip else [(CHIPS, 3, 128, WIDTH)] * CORES
    return pl.pallas_call(
        backward_kernel,
        out_shape=[jax.ShapeDtypeStruct(x, jnp.bfloat16) for x in outs],
        grid_spec=pltpu.PrefetchScalarGridSpec(
            num_scalar_prefetch=1,
            grid=(BLOCKS,),
            in_specs=[spec for _, spec in pieces]
            + [whole((3, PEERS, 128, WIDTH)), kept_spec, kept_spec],
            out_specs=[whole(x) for x in outs],
            scratch_shapes=[
                pltpu.VMEM((ROWS, ROWS), jnp.bfloat16),
                pltpu.VMEM((1, PEERS, 128, WIDTH), jnp.bfloat16),
                pltpu.VMEM((HP, count, HEAD_DIM), jnp.bfloat16),
                pltpu.VMEM((HP, count, HEAD_DIM), jnp.float32),
                pltpu.VMEM((HP, count, HEAD_DIM), jnp.float32),
            ],
        ),
        compiler_params=pltpu.CompilerParams(vmem_limit_bytes=VMEM),
        cost_estimate=cost(10),
    )(scalars, *[x for x, _ in pieces], *saved)


def at_index(x, index):
    shape = x.shape[1:]
    return x, pl.BlockSpec((1,) + shape, lambda i, u: (index,) + (0,) * len(shape))


def at_slab(x, index, slab):
    shape = x.shape[2:]
    return x, pl.BlockSpec((1, 1) + shape, lambda i, u: (index, slab, 0, 0))


def at_core(x):
    return x, pl.BlockSpec(x.shape[:2] + (WIDTH,), lambda i, u: (0, 0, u[1]))


def document_scalars(lengths, count):
    firsts = jnp.cumsum(lengths) - lengths
    places = jnp.arange(0, count, ROWS, dtype=jnp.int32)
    start = jnp.max(jnp.where(firsts[None, :] <= places[:, None], firsts[None, :], 0), axis=1)
    units = jnp.clip((places + ROWS) // 128 - start // 128, 2, 6)
    return jnp.concatenate([units, firsts]).astype(jnp.int32)


def local(queries, keys, values, grad_mixed, doc_lengths, owner):
    rows, width = queries.shape
    group = lax.axis_index("dp")
    groups = lax.axis_size("dp")

    lengths = lax.dynamic_index_in_dim(doc_lengths, group, 0, keepdims=False)
    y, c = position()
    scalars = jnp.concatenate(
        [jnp.stack([y, c]).astype(jnp.int32), document_scalars(lengths, rows * PEERS)]
    )
    ids = jnp.arange(groups, dtype=jnp.int32)
    sender = jnp.sum(jnp.where(owner[None, :] == ids[:, None], ids[None, :], 0), axis=1)
    sender = jnp.clip(sender, 0, groups - 1)

    inputs = [queries, keys, values, grad_mixed]

    first = turn_all(pack_chips(inputs[:3], 0))
    slabs = [(0, 1), (1, 1), (2, 1), (3, 0), (3, 1)]
    swapped = swap_cores(pack_other_core(inputs, slabs))
    second, cotangents = merge_columns(inputs, swapped, slabs, 3)
    second, cotangents = turn_all(second), turn_all(cotangents)
    other = swap_cores(pick_other_core_columns(first))

    pieces = [
        [at_core(x) for x in first] + [at_index(other, d) for d in range(CHIPS)],
        [at_index(x, core) for core in range(CORES) for x in second],
    ]
    spread, saved = [], []
    for k in range(CHUNKS):
        out, *kept = forward(pieces[k], scalars)
        saved.append(kept)
        x = lax.all_to_all(
            out.reshape(groups * PEERS, 16, HEAD_DIM), ("dp", "seq"),
            split_axis=0, concat_axis=0, tiled=True,
        )
        spread.append(x.reshape(groups, PEERS, 16, HEAD_DIM))

    slots = pick(spread, sender)
    landed = lax.all_to_all(slots, "dp", split_axis=0, concat_axis=0, tiled=True)
    mixed = settle(landed)

    def cotangent(k):
        return [at_slab(x, core, k) for core in range(CORES) for x in cotangents]

    got = turn_all(backward(cotangent(0), saved[0], scalars, True))
    other = swap_cores(pick_other_core_rows(got))
    grads = unpack([(x, 0) for x in got], [(other, d) for d in range(CHIPS)], None, 0)

    own, sib = backward(cotangent(1), saved[1], scalars, False)
    sib = swap_cores(sib)
    got = [turn(x, d) for d, x in zip((1, 2, 3), merge_rows(own, sib))]
    grads = unpack(
        [(own, 0)] + [(x, 0) for x in got], [(sib, 0)] + [(x, 1) for x in got], grads, 1
    )
    return (mixed, grads[0], grads[1], grads[2])


def solution(mesh):
    placed = P(("dp", "seq"), None)
    return jax.shard_map(
        local,
        mesh=mesh,
        in_specs=(placed,) * 4 + (P(), P()),
        out_specs=(placed,) * 4,
        check_vma=False,
    )
```

```python
import functools

import jax
import jax.numpy as jnp
from jax import lax
from jax.experimental import pallas as pl
from jax.experimental.pallas import tpu as pltpu
from jax.sharding import PartitionSpec as P

HEAD_DIM = 128
LOG2E = 1.4426950408889634
SCALE = HEAD_DIM ** (-0.5)
ROWS = 256
CHIPS, CORES = 4, 2
PEERS = CHIPS * CORES
CHUNKS = 2
HP = 2
WIDTH = HP * HEAD_DIM
BLOCKS = PEERS * 128 // ROWS
DOCS = 8
FIRSTS = 2 + BLOCKS
REACH = FIRSTS + DOCS
PARTS = 3
KEPT = (BLOCKS, ROWS, ROWS)
NT = (((1,), (1,)), ((), ()))
TN = (((0,), (0,)), ((), ()))
ANY = pl.BlockSpec(memory_space=pl.ANY)
MIB = 1024 * 1024
VMEM = 62 * MIB


def position():
    me = lax.axis_index("seq")
    return lax.div(me, CORES), lax.rem(me, CORES)


def chip(y, d):
    return lax.rem(y + d + CHIPS, CHIPS)


def column(y, c, k):
    return pl.multiple_of((y * CHUNKS + k) * CORES * WIDTH + c * WIDTH, WIDTH)


def turn(x, d):
    pairs = [(i, (i // CORES + d) % CHIPS * CORES + i % CORES) for i in range(PEERS)]
    return lax.ppermute(x, "seq", pairs)


def swap_cores(x):
    return lax.ppermute(x, "seq", [(i, i ^ 1) for i in range(PEERS)])


def turn_all(xs):
    got = {d: turn(xs[d], d) for d in (1, 3, 2)}
    return [xs[0], got[1], got[2], got[3]]


TOKEN = jax.ShapeDtypeStruct((8, 128), jnp.float32)


def cost(microseconds):
    return pl.CostEstimate(
        flops=int(microseconds * 1.1e9), bytes_accessed=MIB // 16, transcendentals=0
    )


def run_two_stages(into_vmem, out_of):
    for x in into_vmem:
        x.start()
    for x, nexts in zip(into_vmem, out_of):
        x.wait()
        for z in nexts:
            z.start()
    for nexts in out_of:
        for z in nexts:
            z.wait()


def copy_kernel(plan, inputs, shapes, pieces, after):
    n, m = len(inputs), len(pieces)

    def kernel(*refs):
        pairs = plan(refs[:n], refs[n + len(after) : -3 - m])
        held, arrive, leave = refs[-2 - m : -2], refs[-2], refs[-1]
        assert len(pairs) == m
        run_two_stages(
            [pltpu.make_async_copy(a, held[i], arrive.at[i]) for i, (a, _) in enumerate(pairs)],
            [[pltpu.make_async_copy(held[i], b, leave.at[i])] for i, (_, b) in enumerate(pairs)],
        )

    *outs, token = pl.pallas_call(
        kernel,
        out_shape=[jax.ShapeDtypeStruct(x, jnp.bfloat16) for x in shapes] + [TOKEN],
        in_specs=[ANY] * (n + len(after)),
        out_specs=[ANY] * (len(shapes) + 1),
        scratch_shapes=[pltpu.VMEM(x, jnp.bfloat16) for x in pieces]
        + [pltpu.SemaphoreType.DMA((m,)), pltpu.SemaphoreType.DMA((m,))],
        compiler_params=pltpu.CompilerParams(vmem_limit_bytes=VMEM),
        cost_estimate=cost(0.05),
    )(*inputs, *after)
    return outs, [token]


def gate(x, after):
    def kernel(*refs):
        pass

    return pl.pallas_call(
        kernel,
        out_shape=jax.ShapeDtypeStruct(x.shape, x.dtype),
        in_specs=[ANY] * (1 + len(after)),
        out_specs=ANY,
        input_output_aliases={0: 0},
        compiler_params=pltpu.CompilerParams(vmem_limit_bytes=VMEM),
        cost_estimate=cost(0.05),
    )(x, *after)


def pack(arrays, k, slabs, after):
    n, rows = len(arrays) - 1, arrays[0].shape[0]

    def plan(ins, outs):
        y, c = position()
        return [
            (ins[a].at[:, pl.ds(column(chip(y, d), 0, k), CORES * WIDTH)], outs[d].at[a])
            for d in (1, 3, 2, 0)
            for a in range(n)
        ] + [
            (ins[a].at[:, pl.ds(column(chip(y, d), 1 - c, k), WIDTH)], outs[CHIPS].at[d, i])
            for d in range(CHIPS)
            for i, (a, k) in enumerate(slabs)
        ]

    shapes = [(n, rows, CORES * WIDTH)] * CHIPS + [(CHIPS, len(slabs), rows, WIDTH)]
    pieces = [(rows, CORES * WIDTH)] * (CHIPS * n) + [(rows, WIDTH)] * (CHIPS * len(slabs))
    return copy_kernel(plan, arrays, shapes, pieces, after)


def merge_columns(arrays, swapped, slabs, after):
    rows, n = arrays[0].shape[0], len(slabs)

    def plan(ins, outs):
        y, c = position()
        pairs = []
        for d in (1, 3, 2, 0):
            for i, (a, k) in enumerate(slabs):
                src = ins[a].at[:, pl.ds(column(chip(y, d), c, k), WIDTH)]
                pairs.append((src, outs[d].at[0, i]))
            pairs.append((ins[-1].at[d], outs[d].at[1]))
        return pairs

    shapes = [(CORES, n, rows, WIDTH)] * CHIPS
    pieces = ([(rows, WIDTH)] * n + [(n, rows, WIDTH)]) * CHIPS
    return copy_kernel(plan, list(arrays) + [swapped], shapes, pieces, after)


def pick_other_core_columns(got, after):
    n, rows, _ = got[0].shape

    def plan(ins, outs):
        _, c = position()
        first = pl.multiple_of((1 - c) * WIDTH, WIDTH)
        return [(ins[d].at[:, :, pl.ds(first, WIDTH)], outs[0].at[d]) for d in range(CHIPS)]

    return copy_kernel(plan, got, [(CHIPS, n, rows, WIDTH)], [(n, rows, WIDTH)] * CHIPS, after)


def pick_other_core_rows(got, after):
    def plan(ins, outs):
        return [(ins[d].at[1], outs[0].at[d]) for d in range(CHIPS)]

    shape = got[0].shape[1:]
    return copy_kernel(plan, got, [(CHIPS,) + shape], [shape] * CHIPS, after)


def merge_rows(own, swapped, after):
    def plan(ins, outs):
        return [
            (ins[core].at[d], outs[i].at[core]) for i, d in enumerate((1, 2, 3)) for core in (0, 1)
        ]

    shape = own.shape[1:]
    return copy_kernel(plan, [own, swapped], [(CORES,) + shape] * 3, [shape] * 6, after)


def unpack(own, sib, into, k, after):
    flat = list(own) + list(sib)
    arrays = []
    for x, _ in flat:
        if not any(x is z for z in arrays):
            arrays.append(x)
    where = [next(i for i, z in enumerate(arrays) if z is x) for x, _ in flat]
    n, rows, width = arrays[0].shape[-3:]
    olds = [] if into is None else list(into)
    order = [i * CHIPS + d for d in (0, 1, 3, 2) for i in range(CORES)]

    def kernel(*refs):
        ins = refs[: len(arrays)]
        outs = refs[len(arrays) + len(olds) + len(after) : -4]
        held, arrive, leave = refs[-3:]
        y, c = position()
        into_vmem, out_of = [], []
        for i in order:
            core = 1 - c if i >= CHIPS else c
            col = column(chip(y, -(i % CHIPS)), core, k)
            src = ins[where[i]].at[flat[i][1]]
            into_vmem.append(pltpu.make_async_copy(src, held.at[i], arrive.at[i]))
            out_of.append([
                pltpu.make_async_copy(
                    held.at[i, a], outs[a].at[:, pl.ds(col, width)], leave.at[i * n + a]
                )
                for a in range(n)
            ])
        run_two_stages(into_vmem, out_of)

    *outs, token = pl.pallas_call(
        kernel,
        out_shape=[jax.ShapeDtypeStruct((rows, PEERS * CHUNKS * WIDTH), jnp.bfloat16)] * n
        + [TOKEN],
        in_specs=[ANY] * (len(arrays) + len(olds) + len(after)),
        out_specs=[ANY] * (n + 1),
        scratch_shapes=[
            pltpu.VMEM((PEERS, n, rows, width), jnp.bfloat16),
            pltpu.SemaphoreType.DMA((PEERS,)),
            pltpu.SemaphoreType.DMA((PEERS * n,)),
        ],
        compiler_params=pltpu.CompilerParams(vmem_limit_bytes=VMEM),
        input_output_aliases={len(arrays) + a: a for a in range(len(olds))},
        cost_estimate=cost(0.05),
    )(*arrays, *olds, *after)
    return outs, [token]


def pick(parts, sender, after):
    groups = parts[0].shape[0]
    n = len(parts)

    def kernel(sender_ref, *refs):
        ins, out, (held, arrive, leave) = refs[:n], refs[n + len(after)], refs[-3:]
        into_vmem, out_of = [], []
        for g in range(groups):
            for k in range(n):
                i = g * n + k
                into_vmem.append(
                    pltpu.make_async_copy(ins[k].at[sender_ref[g]], held.at[i], arrive.at[i])
                )
                out_of.append([pltpu.make_async_copy(held.at[i], out.at[g, k], leave.at[i])])
        run_two_stages(into_vmem, out_of)

    slots, token = pl.pallas_call(
        kernel,
        out_shape=[jax.ShapeDtypeStruct((groups, n) + parts[0].shape[1:], jnp.bfloat16), TOKEN],
        grid_spec=pltpu.PrefetchScalarGridSpec(
            num_scalar_prefetch=1,
            grid=(1,),
            in_specs=[ANY] * (n + len(after)),
            out_specs=[ANY, ANY],
            scratch_shapes=[
                pltpu.VMEM((groups * n,) + parts[0].shape[1:], jnp.bfloat16),
                pltpu.SemaphoreType.DMA((groups * n,)),
                pltpu.SemaphoreType.DMA((groups * n,)),
            ],
        ),
        compiler_params=pltpu.CompilerParams(vmem_limit_bytes=VMEM),
        cost_estimate=cost(0.05),
    )(sender, *parts, *after)
    return slots, [token]


def settle(landed):
    _, peers, chunks, small, lanes = landed.shape
    groups = 8
    heads = landed.shape[0] // groups
    x = landed.reshape(heads, groups, peers, chunks, small, lanes)
    half = groups // 2

    def kernel(x_ref, o_ref):
        for s in range(peers):
            for k in range(chunks):
                for h in range(heads):
                    chip_, core = divmod(s, CORES)
                    col = (((chip_ * chunks + k) * CORES + core) * heads + h) * lanes
                    o_ref[:, col : col + lanes] = x_ref[h, :, s, k].reshape(half * small, lanes)

    return pl.pallas_call(
        kernel,
        out_shape=jax.ShapeDtypeStruct((groups * small, peers * chunks * heads * lanes), jnp.bfloat16),
        grid=(2,),
        in_specs=[
            pl.BlockSpec((heads, half, peers, chunks, small, lanes), lambda i: (0, i, 0, 0, 0, 0))
        ],
        out_specs=pl.BlockSpec((half * small, peers * chunks * heads * lanes), lambda i: (i, 0)),
        compiler_params=pltpu.CompilerParams(vmem_limit_bytes=VMEM),
    )(x)


def triangle(after):
    a = lax.broadcasted_iota(jnp.int32, (ROWS, ROWS), 0)
    b = lax.broadcasted_iota(jnp.int32, (ROWS, ROWS), 1)
    return jnp.where((a > b) if after else (a < b), 1.0, 0.0).astype(jnp.bfloat16)


def key_chunks(units):
    edges = list(range(units * 128, 0, -ROWS)) + [0]
    return [(edges[i + 1], edges[i]) for i in range(len(edges) - 1)]


def gather_rows(pieces, scratch, scalars_ref):
    y, c = scalars_ref[0], scalars_ref[1]
    for i, ref in enumerate(pieces):
        p = chip(y, -(i % CHIPS)) * CORES + (1 - c if i >= CHIPS else c)
        x = ref[...]
        scratch[:, pl.ds(p, 1)] = x.reshape((scratch.shape[0], 1) + scratch.shape[2:])


def row_block(scalars_ref, body):
    i = pl.program_id(0)
    r0 = pl.multiple_of(i * ROWS, ROWS)
    for n in range(2, 7):
        @pl.when(scalars_ref[2 + i] == n)
        def _():
            body(n, r0)


def rows_of(ref, a, first, count, h):
    x = ref[a, pl.ds(first // 128, count // 128), :, h * HEAD_DIM : (h + 1) * HEAD_DIM]
    return x.reshape(count, HEAD_DIM)


def forward_kernel(scalars_ref, *refs):
    pieces = refs[:PEERS]
    out_ref, qkv_ref = refs[-10:-8]
    w_ref, sig_ref, tri_ref = refs[-8:-5], refs[-5:-2], refs[-1]
    heads = range(HP)

    @pl.when(pl.program_id(0) == 0)
    def _():
        tri_ref[...] = triangle(True)
        gather_rows(pieces, qkv_ref, scalars_ref)

    def body(units, r0):
        c0 = pl.multiple_of(r0 + ROWS - units * 128, 128)
        row = lax.broadcasted_iota(jnp.int32, (ROWS, 1), 0) + (r0 - c0)
        start = jnp.zeros((ROWS, 1), jnp.int32) - c0
        for d in range(DOCS):
            first = scalars_ref[FIRSTS + d] - c0
            start = jnp.where(row >= first, jnp.maximum(start, first), start)
        q = [rows_of(qkv_ref, 0, r0, ROWS, h) for h in heads]
        rest = [jnp.zeros((ROWS, 1), jnp.float32)] * HP
        out = [jnp.zeros((ROWS, HEAD_DIM), jnp.float32)] * HP
        for part, (lo, hi) in enumerate(key_chunks(units)):
            n = hi - lo
            col = lax.broadcasted_iota(jnp.int32, (ROWS, n), 1) + lo
            allowed = (col >= start) & (col < row)
            for h in heads:
                k = rows_of(qkv_ref, 1, c0 + lo, n, h)
                v = rows_of(qkv_ref, 2, c0 + lo, n, h)
                t = lax.dot_general(q[h], k, NT, preferred_element_type=jnp.float32)
                t = jnp.where(allowed, t * (SCALE * LOG2E), -1e30)
                tail = jnp.log2(1.0 + jnp.exp2(-jnp.abs(t)))
                z = jnp.maximum(t, 0.0) + tail
                ls = jnp.minimum(t, 0.0) - tail
                after = jnp.dot(
                    z.astype(jnp.bfloat16), tri_ref[:n, :n], preferred_element_type=jnp.float32
                ) + rest[h]
                rest[h] = after[:, :1] + z[:, :1]
                w = jnp.exp2(ls - after).astype(jnp.bfloat16)
                out[h] += jnp.dot(w, v, preferred_element_type=jnp.float32)
                w_ref[part][h, 0, :, :n] = w
                sig_ref[part][h, 0, :, :n] = jnp.exp2(ls).astype(jnp.bfloat16)
        for h in heads:
            x = out[h].astype(jnp.bfloat16)
            for r in range(ROWS // 128):
                for g in range(8):
                    at = r * 128 + g * 16
                    out_ref[h * 8 + g, pl.ds(r0 // 128 + r, 1), 0] = x[at : at + 16].reshape(
                        1, 16, HEAD_DIM
                    )

    row_block(scalars_ref, body)


def backward_kernel(by_chip, scalars_ref, *refs):
    pieces, qkv_ref, refs = refs[:PEERS], refs[PEERS], refs[PEERS + 1 :]
    w_ref, sig_ref = refs[:PARTS], refs[PARTS : 2 * PARTS]
    outs = refs[-6 - (CHIPS if by_chip else CORES) : -6]
    tri_ref, g_ref, dq_ref, dk_acc, dv_acc = refs[-5:]
    heads = range(HP)

    @pl.when(pl.program_id(0) == 0)
    def _():
        tri_ref[...] = triangle(False)
        gather_rows(pieces, g_ref, scalars_ref)
        dk_acc[...] = jnp.zeros_like(dk_acc)
        dv_acc[...] = jnp.zeros_like(dv_acc)

    def body(units, r0):
        c0 = pl.multiple_of(r0 + ROWS - units * 128, 128)
        q = [rows_of(qkv_ref, 0, r0, ROWS, h) for h in heads]
        g = [rows_of(g_ref, 0, r0, ROWS, h) for h in heads]
        upto = [jnp.zeros((ROWS, 1), jnp.float32)] * HP
        dq = [jnp.zeros((ROWS, HEAD_DIM), jnp.float32)] * HP
        for part, (lo, hi) in reversed(list(enumerate(key_chunks(units)))):
            n = hi - lo
            here = pl.ds(pl.multiple_of(c0 + lo, 128), n)
            for h in heads:
                k = rows_of(qkv_ref, 1, c0 + lo, n, h)
                v = rows_of(qkv_ref, 2, c0 + lo, n, h)
                w = w_ref[part][h, 0, :, :n]
                dv_acc[h, here] += lax.dot_general(
                    w, g[h], TN, preferred_element_type=jnp.float32
                )
                dw = lax.dot_general(g[h], v, NT, preferred_element_type=jnp.float32)
                a = w.astype(jnp.float32) * dw
                total = jnp.dot(
                    a.astype(jnp.bfloat16), tri_ref[:n, :n], preferred_element_type=jnp.float32
                ) + (a + upto[h])
                upto[h] = total[:, n - 1 :]
                ds = a - sig_ref[part][h, 0, :, :n].astype(jnp.float32) * total
                ds = ds.astype(jnp.bfloat16)
                dq[h] += jnp.dot(ds, k, preferred_element_type=jnp.float32)
                dk_acc[h, here] += lax.dot_general(
                    ds, q[h], TN, preferred_element_type=jnp.float32
                )
        for h in heads:
            dq_ref[h, pl.ds(r0, ROWS)] = (dq[h] * SCALE).astype(jnp.bfloat16)

    row_block(scalars_ref, body)

    @pl.when(pl.program_id(0) == BLOCKS - 1)
    def _():
        y, c = scalars_ref[0], scalars_ref[1]
        for i in range(PEERS):
            d, sib = i % CHIPS, i // CHIPS
            ref = outs[d].at[sib] if by_chip else outs[sib].at[d]
            p = chip(y, d) * CORES + (1 - c if sib else c)
            at = pl.ds(pl.multiple_of(p * 128, 128), 128)
            for h in heads:
                cols = slice(h * HEAD_DIM, (h + 1) * HEAD_DIM)
                ref[0, :, cols] = dq_ref[h, at]
                ref[1, :, cols] = (dk_acc[h, at] * SCALE).astype(jnp.bfloat16)
                ref[2, :, cols] = dv_acc[h, at].astype(jnp.bfloat16)


def kept_specs():
    return [
        pl.BlockSpec(
            (HP, 1) + KEPT[1:],
            functools.partial(lambda p, i, u: (0, u[REACH + p * BLOCKS + i], 0, 0), part),
        )
        for part in range(PARTS)
    ] * 2


def whole(shape):
    return pl.BlockSpec(shape, lambda i, u: (0,) * len(shape))


def forward(pieces, scalars, shared, k, after):
    kept = jax.ShapeDtypeStruct((HP,) + KEPT, jnp.bfloat16)
    out, qkv = (HP * 8, PEERS, CHUNKS, 16, HEAD_DIM), (3, PEERS, 128, WIDTH)
    out_spec = pl.BlockSpec((HP * 8, PEERS, 1, 16, HEAD_DIM), lambda i, u: (0, 0, k, 0, 0))
    olds = [] if shared is None else [shared]
    out, *saved, token = pl.pallas_call(
        forward_kernel,
        out_shape=[jax.ShapeDtypeStruct(x, jnp.bfloat16) for x in (out, qkv)]
        + [kept] * (2 * PARTS)
        + [TOKEN],
        grid_spec=pltpu.PrefetchScalarGridSpec(
            num_scalar_prefetch=1,
            grid=(BLOCKS,),
            in_specs=[spec for _, spec in pieces] + [ANY] * (len(olds) + len(after)),
            out_specs=[out_spec, whole(qkv)] + kept_specs() + [ANY],
            scratch_shapes=[pltpu.VMEM((ROWS, ROWS), jnp.bfloat16)],
        ),
        compiler_params=pltpu.CompilerParams(vmem_limit_bytes=VMEM),
        input_output_aliases={1 + PEERS: 0} if olds else {},
        cost_estimate=cost(10 if k else 0.05),
    )(scalars, *[x for x, _ in pieces], *olds, *after)
    return out, saved, [token]


def backward(pieces, saved, scalars, by_chip, after):
    count = PEERS * 128
    outs = [(CORES, 3, 128, WIDTH)] * CHIPS if by_chip else [(CHIPS, 3, 128, WIDTH)] * CORES
    *grads, token = pl.pallas_call(
        functools.partial(backward_kernel, by_chip),
        out_shape=[jax.ShapeDtypeStruct(x, jnp.bfloat16) for x in outs] + [TOKEN],
        grid_spec=pltpu.PrefetchScalarGridSpec(
            num_scalar_prefetch=1,
            grid=(BLOCKS,),
            in_specs=[spec for _, spec in pieces]
            + [whole((3, PEERS, 128, WIDTH))]
            + kept_specs()
            + [ANY] * len(after),
            out_specs=[whole(x) for x in outs] + [ANY],
            scratch_shapes=[
                pltpu.VMEM((ROWS, ROWS), jnp.bfloat16),
                pltpu.VMEM((1, PEERS, 128, WIDTH), jnp.bfloat16),
                pltpu.VMEM((HP, count, HEAD_DIM), jnp.bfloat16),
                pltpu.VMEM((HP, count, HEAD_DIM), jnp.float32),
                pltpu.VMEM((HP, count, HEAD_DIM), jnp.float32),
            ],
        ),
        compiler_params=pltpu.CompilerParams(vmem_limit_bytes=VMEM),
        cost_estimate=cost(15),
    )(scalars, *[x for x, _ in pieces], *saved, *after)
    return grads, [token]


def at_index(x, index):
    shape = x.shape[1:]
    return x, pl.BlockSpec((1,) + shape, lambda i, u: (index,) + (0,) * len(shape))


def at_slab(x, index, slab):
    shape = x.shape[2:]
    return x, pl.BlockSpec((1, 1) + shape, lambda i, u: (index, slab, 0, 0))


def at_slabs(x, index, count):
    shape = (1, count) + x.shape[2:]
    return x, pl.BlockSpec(shape, lambda i, u: (index, 0, 0, 0))


def at_core(x):
    return x, pl.BlockSpec(x.shape[:2] + (WIDTH,), lambda i, u: (0, 0, u[1]))


def document_scalars(lengths, count):
    firsts = jnp.cumsum(lengths) - lengths
    places = jnp.arange(0, count, ROWS, dtype=jnp.int32)
    start = jnp.max(jnp.where(firsts[None, :] <= places[:, None], firsts[None, :], 0), axis=1)
    units = jnp.clip((places + ROWS) // 128 - start // 128, 2, 6)
    blocks = jnp.arange(units.shape[0], dtype=jnp.int32)
    reach = [
        lax.cummax(jnp.where(units > 2 * part, blocks, 0), axis=0) for part in range(PARTS)
    ]
    return jnp.concatenate([units, firsts] + reach).astype(jnp.int32)


def local(queries, keys, values, grad_mixed, doc_lengths, owner):
    rows, width = queries.shape
    group = lax.axis_index("dp")
    groups = lax.axis_size("dp")

    lengths = lax.dynamic_index_in_dim(doc_lengths, group, 0, keepdims=False)
    y, c = position()
    scalars = jnp.concatenate(
        [jnp.stack([y, c]).astype(jnp.int32), document_scalars(lengths, rows * PEERS)]
    )
    ids = jnp.arange(groups, dtype=jnp.int32)
    sender = jnp.sum(jnp.where(owner[None, :] == ids[:, None], ids[None, :], 0), axis=1)
    sender = jnp.clip(sender, 0, groups - 1)

    inputs = [queries, keys, values, grad_mixed]

    def cotangent(k):
        return [at_slab(x, core, 3 + k) for core in range(CORES) for x in second]

    slabs = [(0, 1), (1, 1), (2, 1), (3, 0), (3, 1)]
    (*first, other), token = pack(inputs, 0, slabs, [])
    first = turn_all(first)
    swapped = swap_cores(other)
    second, token = merge_columns(inputs, swapped, slabs, token)
    second = turn_all(second)
    (other,), token = pick_other_core_columns(first, token)
    other = swap_cores(other)

    pieces = [at_core(x) for x in first] + [at_index(other, d) for d in range(CHIPS)]
    out, saved0, token = forward(pieces, scalars, None, 0, token)
    pieces = [at_slabs(x, core, 3) for core in range(CORES) for x in second]
    out, saved1, token = forward(pieces, scalars, out, 1, token)

    spread = lax.all_to_all(
        out.reshape(groups * PEERS * CHUNKS, 16, HEAD_DIM),
        ("dp", "seq"), split_axis=0, concat_axis=0, tiled=True,
    )

    got, token = backward(cotangent(0), saved0, scalars, True, token)
    got = turn_all(got)
    (own, sib), token = backward(cotangent(1), saved1, scalars, False, token)

    slots, token = pick([spread.reshape(groups, PEERS * CHUNKS, 16, HEAD_DIM)], sender, token)
    landed = lax.all_to_all(slots, "dp", split_axis=0, concat_axis=0, tiled=True)
    landed = landed.reshape(groups, PEERS, CHUNKS, 16, HEAD_DIM)

    sib = swap_cores(gate(sib, token + got[1:]))
    merged, token = merge_rows(own, sib, token)
    merged = [turn(x, d) for d, x in zip((1, 2, 3), merged)]
    (other,), token = pick_other_core_rows(got, token)
    other = swap_cores(other)
    grads, token = unpack(
        [(x, 0) for x in got], [(other, d) for d in range(CHIPS)], None, 0, token
    )
    grads, token = unpack(
        [(own, 0)] + [(x, 0) for x in merged], [(sib, 0)] + [(x, 1) for x in merged],
        grads, 1, token,
    )
    mixed = settle(landed)
    return (mixed, grads[0], grads[1], grads[2])


def solution(mesh):
    placed = P(("dp", "seq"), None)
    return jax.shard_map(
        local,
        mesh=mesh,
        in_specs=(placed,) * 4 + (P(), P()),
        out_specs=(placed,) * 4,
        check_vma=False,
    )
```

```python
import functools

import jax
import jax.numpy as jnp
from jax import lax
from jax.experimental import pallas as pl
from jax.experimental.pallas import tpu as pltpu
from jax.sharding import PartitionSpec as P

HEAD_DIM = 128
LOG2E = 1.4426950408889634
SCALE = HEAD_DIM ** (-0.5)
ROWS = 256
CHIPS, CORES = 4, 2
PEERS = CHIPS * CORES
CHUNKS = 2
HP = 2
WIDTH = HP * HEAD_DIM
BLOCKS = PEERS * 128 // ROWS
DOCS = 8
FIRSTS = 2 + BLOCKS
REACH = FIRSTS + DOCS
PARTS = 3
KEPT = (BLOCKS, ROWS, ROWS)
NT = (((1,), (1,)), ((), ()))
TN = (((0,), (0,)), ((), ()))
ANY = pl.BlockSpec(memory_space=pl.ANY)
MIB = 1024 * 1024
VMEM = 62 * MIB


def position():
    me = lax.axis_index("seq")
    return lax.div(me, CORES), lax.rem(me, CORES)


def chip(y, d):
    return lax.rem(y + d + CHIPS, CHIPS)


def column(y, c, k):
    return pl.multiple_of((y * CHUNKS + k) * CORES * WIDTH + c * WIDTH, WIDTH)


def turn(x, d):
    pairs = [(i, (i // CORES + d) % CHIPS * CORES + i % CORES) for i in range(PEERS)]
    return lax.ppermute(x, "seq", pairs)


def swap_cores(x):
    return lax.ppermute(x, "seq", [(i, i ^ 1) for i in range(PEERS)])


def turn_across(x, d):
    pairs = [(i, (i // CORES + d) % CHIPS * CORES + 1 - i % CORES) for i in range(PEERS)]
    return lax.ppermute(x, "seq", pairs)


def turn_direct(parts):
    own, sib = list(parts[:CHIPS]), list(parts[CHIPS:])
    sib[0] = turn_across(sib[0], 0)
    for d in (1, 3, 2):
        own[d], sib[d] = turn(own[d], d), turn_across(sib[d], d)
    return own, sib


def turn_all(xs):
    got = {d: turn(xs[d], d) for d in (1, 3, 2)}
    return [xs[0], got[1], got[2], got[3]]


TOKEN = jax.ShapeDtypeStruct((8, 128), jnp.float32)


def cost(microseconds):
    return pl.CostEstimate(
        flops=int(microseconds * 1.1e9), bytes_accessed=MIB // 16, transcendentals=0
    )


def run_two_stages(into_vmem, out_of):
    for x in into_vmem:
        x.start()
    for x, nexts in zip(into_vmem, out_of):
        x.wait()
        for z in nexts:
            z.start()
    for nexts in out_of:
        for z in nexts:
            z.wait()


def copy_kernel(plan, inputs, shapes, pieces, after):
    n, m = len(inputs), len(pieces)

    def kernel(*refs):
        pairs = plan(refs[:n], refs[n + len(after) : -3 - m])
        held, arrive, leave = refs[-2 - m : -2], refs[-2], refs[-1]
        assert len(pairs) == m
        run_two_stages(
            [pltpu.make_async_copy(a, held[i], arrive.at[i]) for i, (a, _) in enumerate(pairs)],
            [[pltpu.make_async_copy(held[i], b, leave.at[i])] for i, (_, b) in enumerate(pairs)],
        )

    *outs, token = pl.pallas_call(
        kernel,
        out_shape=[jax.ShapeDtypeStruct(x, jnp.bfloat16) for x in shapes] + [TOKEN],
        in_specs=[ANY] * (n + len(after)),
        out_specs=[ANY] * (len(shapes) + 1),
        scratch_shapes=[pltpu.VMEM(x, jnp.bfloat16) for x in pieces]
        + [pltpu.SemaphoreType.DMA((m,)), pltpu.SemaphoreType.DMA((m,))],
        compiler_params=pltpu.CompilerParams(vmem_limit_bytes=VMEM),
        cost_estimate=cost(0.05),
    )(*inputs, *after)
    return outs, [token]


def gate(xs, after):
    def kernel(*refs):
        pass

    return pl.pallas_call(
        kernel,
        out_shape=[jax.ShapeDtypeStruct(x.shape, x.dtype) for x in xs],
        in_specs=[ANY] * (len(xs) + len(after)),
        out_specs=[ANY] * len(xs),
        input_output_aliases={i: i for i in range(len(xs))},
        compiler_params=pltpu.CompilerParams(vmem_limit_bytes=VMEM),
        cost_estimate=cost(0.05),
    )(*xs, *after)


def pack(arrays, k, slabs, after):
    n, rows = len(arrays), arrays[0].shape[0]

    def plan(ins, outs):
        y, c = position()
        return [
            (
                ins[a].at[:, pl.ds(column(chip(y, d), 1 - c if sib else c, k), WIDTH)],
                outs[sib * CHIPS + d].at[a],
            )
            for d in (1, 3, 0, 2)
            for sib in range(CORES)
            for a in range(n)
        ] + [
            (ins[a].at[:, pl.ds(column(chip(y, d), 1 - c, k), WIDTH)], outs[PEERS].at[d, i])
            for d in range(CHIPS)
            for i, (a, k) in enumerate(slabs)
        ]

    shapes = [(n, rows, WIDTH)] * PEERS + [(CHIPS, len(slabs), rows, WIDTH)]
    pieces = [(rows, WIDTH)] * (PEERS * n + CHIPS * len(slabs))
    return copy_kernel(plan, arrays, shapes, pieces, after)


def merge_columns(arrays, swapped, slabs, after):
    rows, n = arrays[0].shape[0], len(slabs)

    def plan(ins, outs):
        y, c = position()
        pairs = []
        for d in (1, 3, 2, 0):
            for i, (a, k) in enumerate(slabs):
                src = ins[a].at[:, pl.ds(column(chip(y, d), c, k), WIDTH)]
                pairs.append((src, outs[d].at[0, i]))
            pairs.append((ins[-1].at[d], outs[d].at[1]))
        return pairs

    shapes = [(CORES, n, rows, WIDTH)] * CHIPS
    pieces = ([(rows, WIDTH)] * n + [(n, rows, WIDTH)]) * CHIPS
    return copy_kernel(plan, list(arrays) + [swapped], shapes, pieces, after)


def pick_other_core_rows(got, after):
    def plan(ins, outs):
        return [(ins[d].at[1], outs[0].at[d]) for d in range(CHIPS)]

    shape = got[0].shape[1:]
    return copy_kernel(plan, got, [(CHIPS,) + shape], [shape] * CHIPS, after)


def unpack(own, sib, into, k, after):
    flat = list(own) + list(sib)
    arrays = []
    for x, _ in flat:
        if not any(x is z for z in arrays):
            arrays.append(x)
    where = [next(i for i, z in enumerate(arrays) if z is x) for x, _ in flat]
    n, rows, width = arrays[0].shape[-3:]
    olds = [] if into is None else list(into)
    order = [i * CHIPS + d for d in (0, 1, 3, 2) for i in range(CORES)]

    def kernel(*refs):
        ins = refs[: len(arrays)]
        outs = refs[len(arrays) + len(olds) + len(after) : -4]
        held, arrive, leave = refs[-3:]
        y, c = position()
        into_vmem, out_of = [], []
        for i in order:
            core = 1 - c if i >= CHIPS else c
            col = column(chip(y, -(i % CHIPS)), core, k)
            src = ins[where[i]]
            if flat[i][1] is not None:
                src = src.at[flat[i][1]]
            into_vmem.append(pltpu.make_async_copy(src, held.at[i], arrive.at[i]))
            out_of.append([
                pltpu.make_async_copy(
                    held.at[i, a], outs[a].at[:, pl.ds(col, width)], leave.at[i * n + a]
                )
                for a in range(n)
            ])
        run_two_stages(into_vmem, out_of)

    *outs, token = pl.pallas_call(
        kernel,
        out_shape=[jax.ShapeDtypeStruct((rows, PEERS * CHUNKS * WIDTH), jnp.bfloat16)] * n
        + [TOKEN],
        in_specs=[ANY] * (len(arrays) + len(olds) + len(after)),
        out_specs=[ANY] * (n + 1),
        scratch_shapes=[
            pltpu.VMEM((PEERS, n, rows, width), jnp.bfloat16),
            pltpu.SemaphoreType.DMA((PEERS,)),
            pltpu.SemaphoreType.DMA((PEERS * n,)),
        ],
        compiler_params=pltpu.CompilerParams(vmem_limit_bytes=VMEM),
        input_output_aliases={len(arrays) + a: a for a in range(len(olds))},
        cost_estimate=cost(0.05),
    )(*arrays, *olds, *after)
    return outs, [token]


def pick(parts, sender, after):
    groups = parts[0].shape[0]
    n = len(parts)

    def kernel(sender_ref, *refs):
        ins, out, (held, arrive, leave) = refs[:n], refs[n + len(after)], refs[-3:]
        into_vmem, out_of = [], []
        for g in range(groups):
            for k in range(n):
                i = g * n + k
                into_vmem.append(
                    pltpu.make_async_copy(ins[k].at[sender_ref[g]], held.at[i], arrive.at[i])
                )
                out_of.append([pltpu.make_async_copy(held.at[i], out.at[g, k], leave.at[i])])
        run_two_stages(into_vmem, out_of)

    slots, token = pl.pallas_call(
        kernel,
        out_shape=[jax.ShapeDtypeStruct((groups, n) + parts[0].shape[1:], jnp.bfloat16), TOKEN],
        grid_spec=pltpu.PrefetchScalarGridSpec(
            num_scalar_prefetch=1,
            grid=(1,),
            in_specs=[ANY] * (n + len(after)),
            out_specs=[ANY, ANY],
            scratch_shapes=[
                pltpu.VMEM((groups * n,) + parts[0].shape[1:], jnp.bfloat16),
                pltpu.SemaphoreType.DMA((groups * n,)),
                pltpu.SemaphoreType.DMA((groups * n,)),
            ],
        ),
        compiler_params=pltpu.CompilerParams(vmem_limit_bytes=VMEM),
        cost_estimate=cost(0.05),
    )(sender, *parts, *after)
    return slots, [token]


def settle(landed, after):
    _, peers, chunks, small, lanes = landed.shape
    groups = 8
    heads = landed.shape[0] // groups
    x = landed.reshape(heads, groups, peers, chunks, small, lanes)
    half = groups // 2

    def kernel(x_ref, *refs):
        o_ref = refs[len(after)]
        for s in range(peers):
            for k in range(chunks):
                for h in range(heads):
                    chip_, core = divmod(s, CORES)
                    col = (((chip_ * chunks + k) * CORES + core) * heads + h) * lanes
                    o_ref[:, col : col + lanes] = x_ref[h, :, s, k].reshape(half * small, lanes)

    mixed, token = pl.pallas_call(
        kernel,
        out_shape=[
            jax.ShapeDtypeStruct((groups * small, peers * chunks * heads * lanes), jnp.bfloat16),
            TOKEN,
        ],
        grid=(2,),
        in_specs=[
            pl.BlockSpec((heads, half, peers, chunks, small, lanes), lambda i: (0, i, 0, 0, 0, 0))
        ]
        + [ANY] * len(after),
        out_specs=[
            pl.BlockSpec((half * small, peers * chunks * heads * lanes), lambda i: (i, 0)),
            ANY,
        ],
        compiler_params=pltpu.CompilerParams(vmem_limit_bytes=VMEM),
        cost_estimate=cost(0.05),
    )(x, *after)
    return mixed, [token]


def triangle(after):
    a = lax.broadcasted_iota(jnp.int32, (ROWS, ROWS), 0)
    b = lax.broadcasted_iota(jnp.int32, (ROWS, ROWS), 1)
    return jnp.where((a > b) if after else (a < b), 1.0, 0.0).astype(jnp.bfloat16)


def key_chunks(units):
    edges = list(range(units * 128, 0, -ROWS)) + [0]
    return [(edges[i + 1], edges[i]) for i in range(len(edges) - 1)]


def gather_rows(pieces, scratch, scalars_ref):
    y, c = scalars_ref[0], scalars_ref[1]
    for i, ref in enumerate(pieces):
        p = chip(y, -(i % CHIPS)) * CORES + (1 - c if i >= CHIPS else c)
        x = ref[...]
        scratch[:, pl.ds(p, 1)] = x.reshape((scratch.shape[0], 1) + scratch.shape[2:])


def row_block(scalars_ref, body):
    i = pl.program_id(0)
    r0 = pl.multiple_of(i * ROWS, ROWS)
    for n in range(2, 7):
        @pl.when(scalars_ref[2 + i] == n)
        def _():
            body(n, r0)


def rows_of(ref, a, first, count, h):
    x = ref[a, pl.ds(first // 128, count // 128), :, h * HEAD_DIM : (h + 1) * HEAD_DIM]
    return x.reshape(count, HEAD_DIM)


def forward_kernel(scalars_ref, *refs):
    pieces = refs[:PEERS]
    out_ref, qkv_ref = refs[-10:-8]
    w_ref, sig_ref, tri_ref = refs[-8:-5], refs[-5:-2], refs[-1]
    heads = range(HP)

    @pl.when(pl.program_id(0) == 0)
    def _():
        tri_ref[...] = triangle(True)
        gather_rows(pieces, qkv_ref, scalars_ref)

    def body(units, r0):
        c0 = pl.multiple_of(r0 + ROWS - units * 128, 128)
        row = lax.broadcasted_iota(jnp.int32, (ROWS, 1), 0) + (r0 - c0)
        start = jnp.zeros((ROWS, 1), jnp.int32) - c0
        for d in range(DOCS):
            first = scalars_ref[FIRSTS + d] - c0
            start = jnp.where(row >= first, jnp.maximum(start, first), start)
        q = [rows_of(qkv_ref, 0, r0, ROWS, h) for h in heads]
        rest = [jnp.zeros((ROWS, 1), jnp.float32)] * HP
        out = [jnp.zeros((ROWS, HEAD_DIM), jnp.float32)] * HP
        for part, (lo, hi) in enumerate(key_chunks(units)):
            n = hi - lo
            col = lax.broadcasted_iota(jnp.int32, (ROWS, n), 1) + lo
            allowed = (col >= start) & (col < row)
            for h in heads:
                k = rows_of(qkv_ref, 1, c0 + lo, n, h)
                v = rows_of(qkv_ref, 2, c0 + lo, n, h)
                t = lax.dot_general(q[h], k, NT, preferred_element_type=jnp.float32)
                t = jnp.where(allowed, t * (SCALE * LOG2E), -1e30)
                tail = jnp.log2(1.0 + jnp.exp2(-jnp.abs(t)))
                z = jnp.maximum(t, 0.0) + tail
                ls = jnp.minimum(t, 0.0) - tail
                after = jnp.dot(
                    z.astype(jnp.bfloat16), tri_ref[:n, :n], preferred_element_type=jnp.float32
                ) + rest[h]
                rest[h] = after[:, :1] + z[:, :1]
                w = jnp.exp2(ls - after).astype(jnp.bfloat16)
                out[h] += jnp.dot(w, v, preferred_element_type=jnp.float32)
                w_ref[part][h, 0, :, :n] = w
                sig_ref[part][h, 0, :, :n] = jnp.exp2(ls).astype(jnp.bfloat16)
        for h in heads:
            x = out[h].astype(jnp.bfloat16)
            for r in range(ROWS // 128):
                for g in range(8):
                    at = r * 128 + g * 16
                    out_ref[h * 8 + g, pl.ds(r0 // 128 + r, 1), 0] = x[at : at + 16].reshape(
                        1, 16, HEAD_DIM
                    )

    row_block(scalars_ref, body)


def backward_kernel(by_chip, scalars_ref, *refs):
    pieces, qkv_ref, refs = refs[:PEERS], refs[PEERS], refs[PEERS + 1 :]
    w_ref, sig_ref = refs[:PARTS], refs[PARTS : 2 * PARTS]
    outs = refs[-6 - (CHIPS if by_chip else PEERS) : -6]
    tri_ref, g_ref, dq_ref, dk_acc, dv_acc = refs[-5:]
    heads = range(HP)

    @pl.when(pl.program_id(0) == 0)
    def _():
        tri_ref[...] = triangle(False)
        gather_rows(pieces, g_ref, scalars_ref)
        dk_acc[...] = jnp.zeros_like(dk_acc)
        dv_acc[...] = jnp.zeros_like(dv_acc)

    def body(units, r0):
        c0 = pl.multiple_of(r0 + ROWS - units * 128, 128)
        q = [rows_of(qkv_ref, 0, r0, ROWS, h) for h in heads]
        g = [rows_of(g_ref, 0, r0, ROWS, h) for h in heads]
        upto = [jnp.zeros((ROWS, 1), jnp.float32)] * HP
        dq = [jnp.zeros((ROWS, HEAD_DIM), jnp.float32)] * HP
        for part, (lo, hi) in reversed(list(enumerate(key_chunks(units)))):
            n = hi - lo
            here = pl.ds(pl.multiple_of(c0 + lo, 128), n)
            for h in heads:
                k = rows_of(qkv_ref, 1, c0 + lo, n, h)
                v = rows_of(qkv_ref, 2, c0 + lo, n, h)
                w = w_ref[part][h, 0, :, :n]
                dv_acc[h, here] += lax.dot_general(
                    w, g[h], TN, preferred_element_type=jnp.float32
                )
                dw = lax.dot_general(g[h], v, NT, preferred_element_type=jnp.float32)
                a = w.astype(jnp.float32) * dw
                total = jnp.dot(
                    a.astype(jnp.bfloat16), tri_ref[:n, :n], preferred_element_type=jnp.float32
                ) + (a + upto[h])
                upto[h] = total[:, n - 1 :]
                ds = a - sig_ref[part][h, 0, :, :n].astype(jnp.float32) * total
                ds = ds.astype(jnp.bfloat16)
                dq[h] += jnp.dot(ds, k, preferred_element_type=jnp.float32)
                dk_acc[h, here] += lax.dot_general(
                    ds, q[h], TN, preferred_element_type=jnp.float32
                )
        for h in heads:
            dq_ref[h, pl.ds(r0, ROWS)] = (dq[h] * SCALE).astype(jnp.bfloat16)

    row_block(scalars_ref, body)

    @pl.when(pl.program_id(0) == BLOCKS - 1)
    def _():
        y, c = scalars_ref[0], scalars_ref[1]
        for i in range(PEERS):
            d, sib = i % CHIPS, i // CHIPS
            ref = outs[d].at[sib] if by_chip else outs[i]
            p = chip(y, d) * CORES + (1 - c if sib else c)
            at = pl.ds(pl.multiple_of(p * 128, 128), 128)
            for h in heads:
                cols = slice(h * HEAD_DIM, (h + 1) * HEAD_DIM)
                ref[0, :, cols] = dq_ref[h, at]
                ref[1, :, cols] = (dk_acc[h, at] * SCALE).astype(jnp.bfloat16)
                ref[2, :, cols] = dv_acc[h, at].astype(jnp.bfloat16)


def kept_specs():
    return [
        pl.BlockSpec(
            (HP, 1) + KEPT[1:],
            functools.partial(lambda p, i, u: (0, u[REACH + p * BLOCKS + i], 0, 0), part),
        )
        for part in range(PARTS)
    ] * 2


def whole(shape):
    return pl.BlockSpec(shape, lambda i, u: (0,) * len(shape))


def forward(pieces, scalars, shared, k, after):
    kept = jax.ShapeDtypeStruct((HP,) + KEPT, jnp.bfloat16)
    out, qkv = (HP * 8, PEERS, CHUNKS, 16, HEAD_DIM), (3, PEERS, 128, WIDTH)
    out_spec = pl.BlockSpec((HP * 8, PEERS, 1, 16, HEAD_DIM), lambda i, u: (0, 0, k, 0, 0))
    olds = [] if shared is None else [shared]
    out, *saved, token = pl.pallas_call(
        forward_kernel,
        out_shape=[jax.ShapeDtypeStruct(x, jnp.bfloat16) for x in (out, qkv)]
        + [kept] * (2 * PARTS)
        + [TOKEN],
        grid_spec=pltpu.PrefetchScalarGridSpec(
            num_scalar_prefetch=1,
            grid=(BLOCKS,),
            in_specs=[spec for _, spec in pieces] + [ANY] * (len(olds) + len(after)),
            out_specs=[out_spec, whole(qkv)] + kept_specs() + [ANY],
            scratch_shapes=[pltpu.VMEM((ROWS, ROWS), jnp.bfloat16)],
        ),
        compiler_params=pltpu.CompilerParams(vmem_limit_bytes=VMEM),
        input_output_aliases={1 + PEERS: 0} if olds else {},
        cost_estimate=cost(10 if k else 0.05),
    )(scalars, *[x for x, _ in pieces], *olds, *after)
    return out, saved, [token]


def backward(pieces, saved, scalars, by_chip, after):
    count = PEERS * 128
    outs = [(CORES, 3, 128, WIDTH)] * CHIPS if by_chip else [(3, 128, WIDTH)] * PEERS
    *grads, token = pl.pallas_call(
        functools.partial(backward_kernel, by_chip),
        out_shape=[jax.ShapeDtypeStruct(x, jnp.bfloat16) for x in outs] + [TOKEN],
        grid_spec=pltpu.PrefetchScalarGridSpec(
            num_scalar_prefetch=1,
            grid=(BLOCKS,),
            in_specs=[spec for _, spec in pieces]
            + [whole((3, PEERS, 128, WIDTH))]
            + kept_specs()
            + [ANY] * len(after),
            out_specs=[whole(x) for x in outs] + [ANY],
            scratch_shapes=[
                pltpu.VMEM((ROWS, ROWS), jnp.bfloat16),
                pltpu.VMEM((1, PEERS, 128, WIDTH), jnp.bfloat16),
                pltpu.VMEM((HP, count, HEAD_DIM), jnp.bfloat16),
                pltpu.VMEM((HP, count, HEAD_DIM), jnp.float32),
                pltpu.VMEM((HP, count, HEAD_DIM), jnp.float32),
            ],
        ),
        compiler_params=pltpu.CompilerParams(vmem_limit_bytes=VMEM),
        cost_estimate=cost(15),
    )(scalars, *[x for x, _ in pieces], *saved, *after)
    return grads, [token]


def at_slabs(x, index, first, count):
    shape = (1, count) + x.shape[2:]
    return x, pl.BlockSpec(shape, lambda i, u: (index, first // count, 0, 0))


def at_first(x, first, count):
    return x, pl.BlockSpec((count,) + x.shape[1:], lambda i, u: (first // count, 0, 0))


def document_scalars(lengths, count):
    firsts = jnp.cumsum(lengths) - lengths
    places = jnp.arange(0, count, ROWS, dtype=jnp.int32)
    start = jnp.max(jnp.where(firsts[None, :] <= places[:, None], firsts[None, :], 0), axis=1)
    units = jnp.clip((places + ROWS) // 128 - start // 128, 2, 6)
    blocks = jnp.arange(units.shape[0], dtype=jnp.int32)
    reach = [
        lax.cummax(jnp.where(units > 2 * part, blocks, 0), axis=0) for part in range(PARTS)
    ]
    return jnp.concatenate([units, firsts] + reach).astype(jnp.int32)


def local(queries, keys, values, grad_mixed, doc_lengths, owner):
    rows, width = queries.shape
    group = lax.axis_index("dp")
    groups = lax.axis_size("dp")

    lengths = lax.dynamic_index_in_dim(doc_lengths, group, 0, keepdims=False)
    y, c = position()
    scalars = jnp.concatenate(
        [jnp.stack([y, c]).astype(jnp.int32), document_scalars(lengths, rows * PEERS)]
    )
    ids = jnp.arange(groups, dtype=jnp.int32)
    sender = jnp.sum(jnp.where(owner[None, :] == ids[:, None], ids[None, :], 0), axis=1)
    sender = jnp.clip(sender, 0, groups - 1)

    inputs = [queries, keys, values, grad_mixed]

    slabs = [(a, 1) for a in range(4)]
    (*parts, other), token = pack(inputs, 0, slabs, [])
    own, sib = turn_direct(parts)
    second, token = merge_columns(inputs, swap_cores(other), slabs, token)
    second = turn_all(second)

    pieces = [at_first(x, 0, 3) for x in own + sib]
    out, saved, token = forward(pieces, scalars, None, 0, token)
    pieces = [at_first(x, 3, 1) for x in own + sib]
    got, token = backward(pieces, saved, scalars, True, token)
    got = turn_all(got)

    pieces = [at_slabs(x, core, 0, 3) for core in range(CORES) for x in second]
    out, saved, token = forward(pieces, scalars, out, 1, token)
    spread = lax.all_to_all(
        out.reshape(groups * PEERS * CHUNKS, 16, HEAD_DIM),
        ("dp", "seq"), split_axis=0, concat_axis=0, tiled=True,
    )
    pieces = [at_slabs(x, core, 3, 1) for core in range(CORES) for x in second]
    parts, token = backward(pieces, saved, scalars, False, token)
    parts = gate(parts, token + got[1:])
    own, sib = turn_direct(parts)

    slots, token = pick([spread.reshape(groups, PEERS * CHUNKS, 16, HEAD_DIM)], sender, token)
    landed = lax.all_to_all(slots, "dp", split_axis=0, concat_axis=0, tiled=True)
    landed = landed.reshape(groups, PEERS, CHUNKS, 16, HEAD_DIM)

    near = [own[1], sib[1], own[3], sib[3]]
    (other,), token = pick_other_core_rows(got, token + near)
    other = swap_cores(other)
    grads, token = unpack(
        [(x, 0) for x in got], [(other, d) for d in range(CHIPS)], None, 0, token
    )
    grads, token = unpack([(x, None) for x in own], [(x, None) for x in sib], grads, 1, token)
    mixed, token = settle(landed, token)
    return (mixed, grads[0], grads[1], grads[2])


def solution(mesh):
    placed = P(("dp", "seq"), None)
    return jax.shard_map(
        local,
        mesh=mesh,
        in_specs=(placed,) * 4 + (P(), P()),
        out_specs=(placed,) * 4,
        check_vma=False,
    )
```

```python
import functools

import jax
import jax.numpy as jnp
from jax import lax
from jax.experimental import pallas as pl
from jax.experimental.pallas import tpu as pltpu
from jax.sharding import PartitionSpec as P

HEAD_DIM = 128
LOG2E = 1.4426950408889634
SCALE = HEAD_DIM ** (-0.5)
ROWS = 256
CHIPS, CORES = 4, 2
PEERS = CHIPS * CORES
CHUNKS = 2
HP = 2
WIDTH = HP * HEAD_DIM
BLOCKS = PEERS * 128 // ROWS
DOCS = 8
FIRSTS = 2 + BLOCKS
PARTS = 3
KEPT = (BLOCKS, PARTS, ROWS, ROWS)
NT = (((1,), (1,)), ((), ()))
TN = (((0,), (0,)), ((), ()))
ANY = pl.BlockSpec(memory_space=pl.ANY)
MIB = 1024 * 1024
VMEM = 62 * MIB


def position():
    me = lax.axis_index("seq")
    return lax.div(me, CORES), lax.rem(me, CORES)


def chip(y, d):
    return lax.rem(y + d + CHIPS, CHIPS)


def column(y, c, k):
    return pl.multiple_of((y * CHUNKS + k) * CORES * WIDTH + c * WIDTH, WIDTH)


def turn(x, d):
    pairs = [(i, (i // CORES + d) % CHIPS * CORES + i % CORES) for i in range(PEERS)]
    return lax.ppermute(x, "seq", pairs)


def swap_cores(x):
    return lax.ppermute(x, "seq", [(i, i ^ 1) for i in range(PEERS)])


def turn_across(x, d):
    pairs = [(i, (i // CORES + d) % CHIPS * CORES + 1 - i % CORES) for i in range(PEERS)]
    return lax.ppermute(x, "seq", pairs)


def turn_direct(parts):
    own, sib = list(parts[:CHIPS]), list(parts[CHIPS:])
    sib[0] = turn_across(sib[0], 0)
    for d in (1, 3, 2):
        own[d], sib[d] = turn(own[d], d), turn_across(sib[d], d)
    return own, sib


def turn_all(xs):
    got = {d: turn(xs[d], d) for d in (1, 3, 2)}
    return [xs[0], got[1], got[2], got[3]]


TOKEN = jax.ShapeDtypeStruct((8, 128), jnp.float32)


def cost(microseconds):
    return pl.CostEstimate(
        flops=int(microseconds * 1.1e9), bytes_accessed=MIB // 16, transcendentals=0
    )


def run_two_stages(into_vmem, out_of):
    for x in into_vmem:
        x.start()
    for x, nexts in zip(into_vmem, out_of):
        x.wait()
        for z in nexts:
            z.start()
    for nexts in out_of:
        for z in nexts:
            z.wait()


def copy_kernel(plan, inputs, shapes, pieces, after):
    n, m = len(inputs), len(pieces)

    def kernel(*refs):
        pairs = plan(refs[:n], refs[n + len(after) : -3 - m])
        held, arrive, leave = refs[-2 - m : -2], refs[-2], refs[-1]
        assert len(pairs) == m
        run_two_stages(
            [pltpu.make_async_copy(a, held[i], arrive.at[i]) for i, (a, _) in enumerate(pairs)],
            [[pltpu.make_async_copy(held[i], b, leave.at[i])] for i, (_, b) in enumerate(pairs)],
        )

    *outs, token = pl.pallas_call(
        kernel,
        out_shape=[jax.ShapeDtypeStruct(x, jnp.bfloat16) for x in shapes] + [TOKEN],
        in_specs=[ANY] * (n + len(after)),
        out_specs=[ANY] * (len(shapes) + 1),
        scratch_shapes=[pltpu.VMEM(x, jnp.bfloat16) for x in pieces]
        + [pltpu.SemaphoreType.DMA((m,)), pltpu.SemaphoreType.DMA((m,))],
        compiler_params=pltpu.CompilerParams(vmem_limit_bytes=VMEM),
        cost_estimate=cost(0.05),
    )(*inputs, *after)
    return outs, [token]


def gate(xs, after):
    def kernel(*refs):
        pass

    return pl.pallas_call(
        kernel,
        out_shape=[jax.ShapeDtypeStruct(x.shape, x.dtype) for x in xs],
        in_specs=[ANY] * (len(xs) + len(after)),
        out_specs=[ANY] * len(xs),
        input_output_aliases={i: i for i in range(len(xs))},
        compiler_params=pltpu.CompilerParams(vmem_limit_bytes=VMEM),
        cost_estimate=cost(0.05),
    )(*xs, *after)


def pack(arrays, k, slabs, after):
    n, rows = len(arrays), arrays[0].shape[0]

    def plan(ins, outs):
        y, c = position()
        return [
            (
                ins[a].at[:, pl.ds(column(chip(y, d), 1 - c if sib else c, k), WIDTH)],
                outs[sib * CHIPS + d].at[a],
            )
            for d in (1, 3, 0, 2)
            for sib in range(CORES)
            for a in range(n)
        ] + [
            (ins[a].at[:, pl.ds(column(chip(y, d), 1 - c, k), WIDTH)], outs[PEERS].at[d, i])
            for d in range(CHIPS)
            for i, (a, k) in enumerate(slabs)
        ]

    shapes = [(n, rows, WIDTH)] * PEERS + [(CHIPS, len(slabs), rows, WIDTH)]
    pieces = [(rows, WIDTH)] * (PEERS * n + CHIPS * len(slabs))
    return copy_kernel(plan, arrays, shapes, pieces, after)


def merge_columns(arrays, swapped, slabs, after):
    rows, n = arrays[0].shape[0], len(slabs)

    def plan(ins, outs):
        y, c = position()
        pairs = []
        for d in (1, 3, 2, 0):
            for i, (a, k) in enumerate(slabs):
                src = ins[a].at[:, pl.ds(column(chip(y, d), c, k), WIDTH)]
                pairs.append((src, outs[d].at[0, i]))
            pairs.append((ins[-1].at[d], outs[d].at[1]))
        return pairs

    shapes = [(CORES, n, rows, WIDTH)] * CHIPS
    pieces = ([(rows, WIDTH)] * n + [(n, rows, WIDTH)]) * CHIPS
    return copy_kernel(plan, list(arrays) + [swapped], shapes, pieces, after)


def pick_other_core_rows(got, after):
    def plan(ins, outs):
        return [(ins[d].at[1], outs[0].at[d]) for d in range(CHIPS)]

    shape = got[0].shape[1:]
    return copy_kernel(plan, got, [(CHIPS,) + shape], [shape] * CHIPS, after)


def unpack(own, sib, into, k, after):
    flat = list(own) + list(sib)
    arrays = []
    for x, _ in flat:
        if not any(x is z for z in arrays):
            arrays.append(x)
    where = [next(i for i, z in enumerate(arrays) if z is x) for x, _ in flat]
    n, rows, width = arrays[0].shape[-3:]
    olds = [] if into is None else list(into)
    order = [i * CHIPS + d for d in (0, 1, 3, 2) for i in range(CORES)]

    def kernel(*refs):
        ins = refs[: len(arrays)]
        outs = refs[len(arrays) + len(olds) + len(after) : -4]
        held, arrive, leave = refs[-3:]
        y, c = position()
        into_vmem, out_of = [], []
        for i in order:
            core = 1 - c if i >= CHIPS else c
            col = column(chip(y, -(i % CHIPS)), core, k)
            src = ins[where[i]]
            if flat[i][1] is not None:
                src = src.at[flat[i][1]]
            into_vmem.append(pltpu.make_async_copy(src, held.at[i], arrive.at[i]))
            out_of.append([
                pltpu.make_async_copy(
                    held.at[i, a], outs[a].at[:, pl.ds(col, width)], leave.at[i * n + a]
                )
                for a in range(n)
            ])
        run_two_stages(into_vmem, out_of)

    *outs, token = pl.pallas_call(
        kernel,
        out_shape=[jax.ShapeDtypeStruct((rows, PEERS * CHUNKS * WIDTH), jnp.bfloat16)] * n
        + [TOKEN],
        in_specs=[ANY] * (len(arrays) + len(olds) + len(after)),
        out_specs=[ANY] * (n + 1),
        scratch_shapes=[
            pltpu.VMEM((PEERS, n, rows, width), jnp.bfloat16),
            pltpu.SemaphoreType.DMA((PEERS,)),
            pltpu.SemaphoreType.DMA((PEERS * n,)),
        ],
        compiler_params=pltpu.CompilerParams(vmem_limit_bytes=VMEM),
        input_output_aliases={len(arrays) + a: a for a in range(len(olds))},
        cost_estimate=cost(0.05),
    )(*arrays, *olds, *after)
    return outs, [token]


def pick(parts, sender, after):
    groups = parts[0].shape[0]
    n = len(parts)

    def kernel(sender_ref, *refs):
        ins, out, (held, arrive, leave) = refs[:n], refs[n + len(after)], refs[-3:]
        into_vmem, out_of = [], []
        for g in range(groups):
            for k in range(n):
                i = g * n + k
                into_vmem.append(
                    pltpu.make_async_copy(ins[k].at[sender_ref[g]], held.at[i], arrive.at[i])
                )
                out_of.append([pltpu.make_async_copy(held.at[i], out.at[g, k], leave.at[i])])
        run_two_stages(into_vmem, out_of)

    slots, token = pl.pallas_call(
        kernel,
        out_shape=[jax.ShapeDtypeStruct((groups, n) + parts[0].shape[1:], jnp.bfloat16), TOKEN],
        grid_spec=pltpu.PrefetchScalarGridSpec(
            num_scalar_prefetch=1,
            grid=(1,),
            in_specs=[ANY] * (n + len(after)),
            out_specs=[ANY, ANY],
            scratch_shapes=[
                pltpu.VMEM((groups * n,) + parts[0].shape[1:], jnp.bfloat16),
                pltpu.SemaphoreType.DMA((groups * n,)),
                pltpu.SemaphoreType.DMA((groups * n,)),
            ],
        ),
        compiler_params=pltpu.CompilerParams(vmem_limit_bytes=VMEM),
        cost_estimate=cost(0.05),
    )(sender, *parts, *after)
    return slots, [token]


def settle(landed, after):
    _, peers, chunks, small, lanes = landed.shape
    groups = 8
    heads = landed.shape[0] // groups
    x = landed.reshape(heads, groups, peers, chunks, small, lanes)
    half = groups // 2

    def kernel(x_ref, *refs):
        o_ref = refs[len(after)]
        for s in range(peers):
            for k in range(chunks):
                for h in range(heads):
                    chip_, core = divmod(s, CORES)
                    col = (((chip_ * chunks + k) * CORES + core) * heads + h) * lanes
                    o_ref[:, col : col + lanes] = x_ref[h, :, s, k].reshape(half * small, lanes)

    mixed, token = pl.pallas_call(
        kernel,
        out_shape=[
            jax.ShapeDtypeStruct((groups * small, peers * chunks * heads * lanes), jnp.bfloat16),
            TOKEN,
        ],
        grid=(2,),
        in_specs=[
            pl.BlockSpec((heads, half, peers, chunks, small, lanes), lambda i: (0, i, 0, 0, 0, 0))
        ]
        + [ANY] * len(after),
        out_specs=[
            pl.BlockSpec((half * small, peers * chunks * heads * lanes), lambda i: (i, 0)),
            ANY,
        ],
        compiler_params=pltpu.CompilerParams(vmem_limit_bytes=VMEM),
        cost_estimate=cost(0.05),
    )(x, *after)
    return mixed, [token]


def triangle(after):
    a = lax.broadcasted_iota(jnp.int32, (ROWS, ROWS), 0)
    b = lax.broadcasted_iota(jnp.int32, (ROWS, ROWS), 1)
    return jnp.where((a > b) if after else (a < b), 1.0, 0.0).astype(jnp.bfloat16)


def gather_rows(pieces, scratch, scalars_ref):
    y, c = scalars_ref[0], scalars_ref[1]
    for i, ref in enumerate(pieces):
        p = chip(y, -(i % CHIPS)) * CORES + (1 - c if i >= CHIPS else c)
        x = ref[...]
        scratch[:, pl.ds(p, 1)] = x.reshape((scratch.shape[0], 1) + scratch.shape[2:])


def rows_of(ref, a, first, count, h):
    x = ref[a, pl.ds(first // 128, count // 128), :, h * HEAD_DIM : (h + 1) * HEAD_DIM]
    return x.reshape(count, HEAD_DIM)


def forward_kernel(scalars_ref, *refs):
    pieces = refs[:PEERS]
    out_ref, w_ref, sig_ref, _, tri_ref, acc_ref, qkv_ref = refs[-7:]
    heads = range(HP)
    i = pl.program_id(0)
    r0 = pl.multiple_of(i * ROWS, ROWS)

    @pl.when(i == 0)
    def _():
        tri_ref[...] = triangle(True)
        gather_rows(pieces, qkv_ref, scalars_ref)

    row = lax.broadcasted_iota(jnp.int32, (ROWS, 1), 0) + r0
    start = jnp.zeros((ROWS, 1), jnp.int32)
    for d in range(DOCS):
        first = scalars_ref[FIRSTS + d]
        start = jnp.where(row >= first, jnp.maximum(start, first), start)
    q = [rows_of(qkv_ref, 0, r0, ROWS, h) for h in heads]
    acc_ref[...] = jnp.zeros_like(acc_ref)

    def body(j, rest):
        lo = pl.multiple_of(r0 - j * ROWS, ROWS)
        col = lax.broadcasted_iota(jnp.int32, (ROWS, ROWS), 1) + lo
        allowed = (col >= start) & (col < row)
        left = []
        for h in heads:
            k, v = rows_of(qkv_ref, 1, lo, ROWS, h), rows_of(qkv_ref, 2, lo, ROWS, h)
            t = lax.dot_general(q[h], k, NT, preferred_element_type=jnp.float32)
            t = jnp.where(allowed, t * (SCALE * LOG2E), -1e30)
            tail = jnp.log2(1.0 + jnp.exp2(-jnp.abs(t)))
            z = jnp.maximum(t, 0.0) + tail
            ls = jnp.minimum(t, 0.0) - tail
            after = jnp.dot(
                z.astype(jnp.bfloat16), tri_ref[...], preferred_element_type=jnp.float32
            ) + rest[h]
            left.append(after[:, :1] + z[:, :1])
            w = jnp.exp2(ls - after).astype(jnp.bfloat16)
            acc_ref[h] += jnp.dot(w, v, preferred_element_type=jnp.float32)
            w_ref[h, 0, j] = w
            sig_ref[h, 0, j] = jnp.exp2(ls).astype(jnp.bfloat16)
        return tuple(left)

    lax.fori_loop(0, scalars_ref[2 + i], body, (jnp.zeros((ROWS, 1), jnp.float32),) * HP)

    for h in heads:
        x = acc_ref[h].astype(jnp.bfloat16)
        for r in range(ROWS // 128):
            for g in range(8):
                at = r * 128 + g * 16
                out_ref[h * 8 + g, pl.ds(r0 // 128 + r, 1), 0] = x[at : at + 16].reshape(
                    1, 16, HEAD_DIM
                )


def backward_kernel(by_chip, scalars_ref, *refs):
    pieces, (w_ref, sig_ref) = refs[:PEERS], refs[PEERS : PEERS + 2]
    outs = refs[-7 - (CHIPS if by_chip else PEERS) : -7]
    tri_ref, qkv_ref, dq_ref, acc_ref, dk_acc, dv_acc = refs[-6:]
    heads = range(HP)
    block = pl.program_id(0)
    r0 = pl.multiple_of(block * ROWS, ROWS)

    @pl.when(block == 0)
    def _():
        tri_ref[...] = triangle(False)
        gather_rows(pieces, qkv_ref, scalars_ref)
        dk_acc[...] = jnp.zeros_like(dk_acc)
        dv_acc[...] = jnp.zeros_like(dv_acc)

    q = [rows_of(qkv_ref, 0, r0, ROWS, h) for h in heads]
    g = [rows_of(qkv_ref, 3, r0, ROWS, h) for h in heads]
    acc_ref[...] = jnp.zeros_like(acc_ref)
    chunks = scalars_ref[2 + block]

    def body(i, upto):
        j = chunks - 1 - i
        lo = pl.multiple_of(r0 - j * ROWS, ROWS)
        here = pl.ds(lo, ROWS)
        right = []
        for h in heads:
            k, v = rows_of(qkv_ref, 1, lo, ROWS, h), rows_of(qkv_ref, 2, lo, ROWS, h)
            w = w_ref[h, 0, j]
            dv_acc[h, here] += lax.dot_general(w, g[h], TN, preferred_element_type=jnp.float32)
            dw = lax.dot_general(g[h], v, NT, preferred_element_type=jnp.float32)
            a = w.astype(jnp.float32) * dw
            total = jnp.dot(
                a.astype(jnp.bfloat16), tri_ref[...], preferred_element_type=jnp.float32
            ) + (a + upto[h])
            right.append(total[:, ROWS - 1 :])
            ds = (a - sig_ref[h, 0, j].astype(jnp.float32) * total).astype(jnp.bfloat16)
            acc_ref[h] += jnp.dot(ds, k, preferred_element_type=jnp.float32)
            dk_acc[h, here] += lax.dot_general(ds, q[h], TN, preferred_element_type=jnp.float32)
        return tuple(right)

    lax.fori_loop(0, chunks, body, (jnp.zeros((ROWS, 1), jnp.float32),) * HP)
    for h in heads:
        dq_ref[h, pl.ds(r0, ROWS)] = (acc_ref[h] * SCALE).astype(jnp.bfloat16)

    @pl.when(pl.program_id(0) == BLOCKS - 1)
    def _():
        y, c = scalars_ref[0], scalars_ref[1]
        for i in range(PEERS):
            d, sib = i % CHIPS, i // CHIPS
            ref = outs[d].at[sib] if by_chip else outs[i]
            p = chip(y, d) * CORES + (1 - c if sib else c)
            at = pl.ds(pl.multiple_of(p * 128, 128), 128)
            for h in heads:
                cols = slice(h * HEAD_DIM, (h + 1) * HEAD_DIM)
                ref[0, :, cols] = dq_ref[h, at]
                ref[1, :, cols] = (dk_acc[h, at] * SCALE).astype(jnp.bfloat16)
                ref[2, :, cols] = dv_acc[h, at].astype(jnp.bfloat16)


def kept_spec():
    return pl.BlockSpec((HP, 1) + KEPT[1:], lambda i, u: (0, i, 0, 0, 0))


def whole(shape):
    return pl.BlockSpec(shape, lambda i, u: (0,) * len(shape))


def forward(pieces, scalars, shared, k, after):
    kept = jax.ShapeDtypeStruct((HP,) + KEPT, jnp.bfloat16)
    out = (HP * 8, PEERS, CHUNKS, 16, HEAD_DIM)
    out_spec = pl.BlockSpec((HP * 8, PEERS, 1, 16, HEAD_DIM), lambda i, u: (0, 0, k, 0, 0))
    olds = [] if shared is None else [shared]
    out, *saved, token = pl.pallas_call(
        forward_kernel,
        out_shape=[jax.ShapeDtypeStruct(out, jnp.bfloat16), kept, kept, TOKEN],
        grid_spec=pltpu.PrefetchScalarGridSpec(
            num_scalar_prefetch=1,
            grid=(BLOCKS,),
            in_specs=[spec for _, spec in pieces] + [ANY] * (len(olds) + len(after)),
            out_specs=[out_spec, kept_spec(), kept_spec(), ANY],
            scratch_shapes=[
                pltpu.VMEM((ROWS, ROWS), jnp.bfloat16),
                pltpu.VMEM((HP, ROWS, HEAD_DIM), jnp.float32),
                pltpu.VMEM((3, PEERS, 128, WIDTH), jnp.bfloat16),
            ],
        ),
        compiler_params=pltpu.CompilerParams(vmem_limit_bytes=VMEM),
        input_output_aliases={1 + PEERS: 0} if olds else {},
        cost_estimate=cost(10 if k else 0.05),
    )(scalars, *[x for x, _ in pieces], *olds, *after)
    return out, saved, [token]


def backward(pieces, saved, scalars, by_chip, after):
    count = PEERS * 128
    outs = [(CORES, 3, 128, WIDTH)] * CHIPS if by_chip else [(3, 128, WIDTH)] * PEERS
    *grads, token = pl.pallas_call(
        functools.partial(backward_kernel, by_chip),
        out_shape=[jax.ShapeDtypeStruct(x, jnp.bfloat16) for x in outs] + [TOKEN],
        grid_spec=pltpu.PrefetchScalarGridSpec(
            num_scalar_prefetch=1,
            grid=(BLOCKS,),
            in_specs=[spec for _, spec in pieces]
            + [kept_spec(), kept_spec()]
            + [ANY] * len(after),
            out_specs=[whole(x) for x in outs] + [ANY],
            scratch_shapes=[
                pltpu.VMEM((ROWS, ROWS), jnp.bfloat16),
                pltpu.VMEM((4, PEERS, 128, WIDTH), jnp.bfloat16),
                pltpu.VMEM((HP, count, HEAD_DIM), jnp.bfloat16),
                pltpu.VMEM((HP, ROWS, HEAD_DIM), jnp.float32),
                pltpu.VMEM((HP, count, HEAD_DIM), jnp.float32),
                pltpu.VMEM((HP, count, HEAD_DIM), jnp.float32),
            ],
        ),
        compiler_params=pltpu.CompilerParams(vmem_limit_bytes=VMEM),
        cost_estimate=cost(15),
    )(scalars, *[x for x, _ in pieces], *saved, *after)
    return grads, [token]


def at_slabs(x, index, first, count):
    shape = (1, count) + x.shape[2:]
    return x, pl.BlockSpec(shape, lambda i, u: (index, first // count, 0, 0))


def at_first(x, first, count):
    return x, pl.BlockSpec((count,) + x.shape[1:], lambda i, u: (first // count, 0, 0))


def document_scalars(lengths, count):
    firsts = jnp.cumsum(lengths) - lengths
    places = jnp.arange(0, count, ROWS, dtype=jnp.int32)
    start = jnp.max(jnp.where(firsts[None, :] <= places[:, None], firsts[None, :], 0), axis=1)
    chunks = jnp.clip(places // ROWS - start // ROWS + 1, 1, jnp.minimum(places // ROWS + 1, PARTS))
    return jnp.concatenate([chunks, firsts]).astype(jnp.int32)


def local(queries, keys, values, grad_mixed, doc_lengths, owner):
    rows, width = queries.shape
    group = lax.axis_index("dp")
    groups = lax.axis_size("dp")

    lengths = lax.dynamic_index_in_dim(doc_lengths, group, 0, keepdims=False)
    y, c = position()
    scalars = jnp.concatenate(
        [jnp.stack([y, c]).astype(jnp.int32), document_scalars(lengths, rows * PEERS)]
    )
    ids = jnp.arange(groups, dtype=jnp.int32)
    sender = jnp.sum(jnp.where(owner[None, :] == ids[:, None], ids[None, :], 0), axis=1)
    sender = jnp.clip(sender, 0, groups - 1)

    inputs = [queries, keys, values, grad_mixed]

    slabs = [(a, 1) for a in range(4)]
    (*parts, other), token = pack(inputs, 0, slabs, [])
    own, sib = turn_direct(parts)
    second, token = merge_columns(inputs, swap_cores(other), slabs, token)
    second = turn_all(second)

    pieces = [at_first(x, 0, 3) for x in own + sib]
    out, saved, token = forward(pieces, scalars, None, 0, token)
    pieces = [at_first(x, 0, 4) for x in own + sib]
    got, token = backward(pieces, saved, scalars, True, token)
    got = turn_all(got)

    pieces = [at_slabs(x, core, 0, 3) for core in range(CORES) for x in second]
    out, saved, token = forward(pieces, scalars, out, 1, token)
    spread = lax.all_to_all(
        out.reshape(groups * PEERS * CHUNKS, 16, HEAD_DIM),
        ("dp", "seq"), split_axis=0, concat_axis=0, tiled=True,
    )
    pieces = [at_slabs(x, core, 0, 4) for core in range(CORES) for x in second]
    parts, token = backward(pieces, saved, scalars, False, token)
    parts = gate(parts, token + got[1:])
    own, sib = turn_direct(parts)

    slots, token = pick([spread.reshape(groups, PEERS * CHUNKS, 16, HEAD_DIM)], sender, token)
    landed = lax.all_to_all(slots, "dp", split_axis=0, concat_axis=0, tiled=True)
    landed = landed.reshape(groups, PEERS, CHUNKS, 16, HEAD_DIM)

    near = [own[1], sib[1], own[3], sib[3]]
    (other,), token = pick_other_core_rows(got, token + near)
    other = swap_cores(other)
    grads, token = unpack(
        [(x, 0) for x in got], [(other, d) for d in range(CHIPS)], None, 0, token
    )
    grads, token = unpack([(x, None) for x in own], [(x, None) for x in sib], grads, 1, token)
    mixed, token = settle(landed, token)
    return (mixed, grads[0], grads[1], grads[2])


def solution(mesh):
    placed = P(("dp", "seq"), None)
    return jax.shard_map(
        local,
        mesh=mesh,
        in_specs=(placed,) * 4 + (P(), P()),
        out_specs=(placed,) * 4,
        check_vma=False,
    )
```

```python
import functools

import jax
import jax.numpy as jnp
from jax import lax
from jax.experimental import pallas as pl
from jax.experimental.pallas import tpu as pltpu
from jax.sharding import PartitionSpec as P

HEAD_DIM = 128
LOG2E = 1.4426950408889634
SCALE = HEAD_DIM ** (-0.5)
ROWS = 256
CHIPS, CORES = 4, 2
PEERS = CHIPS * CORES
CHUNKS = 2
HP = 2
WIDTH = HP * HEAD_DIM
BLOCKS = PEERS * 128 // ROWS
DOCS = 8
FIRSTS = 2 + BLOCKS
PARTS = 3
KEPT = (BLOCKS, PARTS, ROWS, ROWS)
NT = (((1,), (1,)), ((), ()))
TN = (((0,), (0,)), ((), ()))
ANY = pl.BlockSpec(memory_space=pl.ANY)
MIB = 1024 * 1024
VMEM = 62 * MIB


def position():
    me = lax.axis_index("seq")
    return lax.div(me, CORES), lax.rem(me, CORES)


def chip(y, d):
    return lax.rem(y + d + CHIPS, CHIPS)


def column(y, c, k):
    return pl.multiple_of((y * CHUNKS + k) * CORES * WIDTH + c * WIDTH, WIDTH)


def turn(x, d):
    pairs = [(i, (i // CORES + d) % CHIPS * CORES + i % CORES) for i in range(PEERS)]
    return lax.ppermute(x, "seq", pairs)


def swap_cores(x):
    return lax.ppermute(x, "seq", [(i, i ^ 1) for i in range(PEERS)])


def turn_across(x, d):
    pairs = [(i, (i // CORES + d) % CHIPS * CORES + 1 - i % CORES) for i in range(PEERS)]
    return lax.ppermute(x, "seq", pairs)


def turn_direct(parts):
    own, sib = list(parts[:CHIPS]), list(parts[CHIPS:])
    for d in (1, 3, 2):
        own[d], sib[d] = turn(own[d], d), turn_across(sib[d], d)
    return own, sib


def turn_all(xs):
    got = {d: turn(xs[d], d) for d in (1, 3, 2)}
    return [xs[0], got[1], got[2], got[3]]


TOKEN = jax.ShapeDtypeStruct((8, 128), jnp.float32)


def cost(microseconds):
    return pl.CostEstimate(
        flops=int(microseconds * 1.1e9), bytes_accessed=MIB // 16, transcendentals=0
    )


def run_two_stages(into_vmem, out_of):
    for x in into_vmem:
        x.start()
    for x, nexts in zip(into_vmem, out_of):
        x.wait()
        for z in nexts:
            z.start()
    for nexts in out_of:
        for z in nexts:
            z.wait()


def copy_kernel(plan, inputs, shapes, pieces, after):
    n, m = len(inputs), len(pieces)

    def kernel(*refs):
        pairs = plan(refs[:n], refs[n + len(after) : -3 - m])
        held, arrive, leave = refs[-2 - m : -2], refs[-2], refs[-1]
        assert len(pairs) == m
        run_two_stages(
            [pltpu.make_async_copy(a, held[i], arrive.at[i]) for i, (a, _) in enumerate(pairs)],
            [[pltpu.make_async_copy(held[i], b, leave.at[i])] for i, (_, b) in enumerate(pairs)],
        )

    *outs, token = pl.pallas_call(
        kernel,
        out_shape=[jax.ShapeDtypeStruct(x, jnp.bfloat16) for x in shapes] + [TOKEN],
        in_specs=[ANY] * (n + len(after)),
        out_specs=[ANY] * (len(shapes) + 1),
        scratch_shapes=[pltpu.VMEM(x, jnp.bfloat16) for x in pieces]
        + [pltpu.SemaphoreType.DMA((m,)), pltpu.SemaphoreType.DMA((m,))],
        compiler_params=pltpu.CompilerParams(vmem_limit_bytes=VMEM),
        cost_estimate=cost(0.05),
    )(*inputs, *after)
    return outs, [token]


def gate(xs, after):
    def kernel(*refs):
        pass

    return pl.pallas_call(
        kernel,
        out_shape=[jax.ShapeDtypeStruct(x.shape, x.dtype) for x in xs],
        in_specs=[ANY] * (len(xs) + len(after)),
        out_specs=[ANY] * len(xs),
        input_output_aliases={i: i for i in range(len(xs))},
        compiler_params=pltpu.CompilerParams(vmem_limit_bytes=VMEM),
        cost_estimate=cost(0.05),
    )(*xs, *after)


def pack(arrays, k, slabs, after):
    n, rows = len(arrays), arrays[0].shape[0]
    parts = [(d, sib) for d in (1, 3, 2, 0) for sib in range(CORES) if (d, sib) != (0, 1)]

    def plan(ins, outs):
        y, c = position()
        return [
            (
                ins[a].at[:, pl.ds(column(chip(y, d), 1 - c if sib else c, k), WIDTH)],
                outs[i].at[a],
            )
            for i, (d, sib) in enumerate(parts)
            for a in range(n)
        ] + [
            (ins[a].at[:, pl.ds(column(chip(y, d), 1 - c, j), WIDTH)], outs[-1].at[o, i])
            for o, d in enumerate(list(range(CHIPS)) + [0])
            for i, (a, j) in enumerate(slabs if o < CHIPS else [(a, k) for a, _ in slabs])
        ]

    shapes = [(n, rows, WIDTH)] * len(parts) + [(CHIPS + 1, len(slabs), rows, WIDTH)]
    pieces = [(rows, WIDTH)] * (len(parts) * n + (CHIPS + 1) * len(slabs))
    (*outs, other), token = copy_kernel(plan, arrays, shapes, pieces, after)
    by_part = dict(zip(parts, outs))
    own = [by_part[d, 0] for d in range(CHIPS)]
    return own + [None] + [by_part[d, 1] for d in (1, 2, 3)], other, token


def merge_columns(arrays, swapped, slabs, after):
    rows, n = arrays[0].shape[0], len(slabs)

    def plan(ins, outs):
        y, c = position()
        pairs = []
        for d in (1, 3, 2, 0):
            for i, (a, k) in enumerate(slabs):
                src = ins[a].at[:, pl.ds(column(chip(y, d), c, k), WIDTH)]
                pairs.append((src, outs[d].at[0, i]))
            pairs.append((ins[-1].at[d], outs[d].at[1]))
        return pairs

    shapes = [(CORES, n, rows, WIDTH)] * CHIPS
    pieces = ([(rows, WIDTH)] * n + [(n, rows, WIDTH)]) * CHIPS
    return copy_kernel(plan, list(arrays) + [swapped], shapes, pieces, after)


def pick_other_core_rows(got, last, after):
    def plan(ins, outs):
        return [(ins[d].at[1], outs[0].at[d]) for d in range(CHIPS)] + [(ins[-1], outs[0].at[CHIPS])]

    shape = got[0].shape[1:]
    inputs = list(got) + [last]
    return copy_kernel(plan, inputs, [(CHIPS + 1,) + shape], [shape] * (CHIPS + 1), after)


def unpack(own, sib, into, k, after):
    flat = list(own) + list(sib)
    arrays = []
    for x, _ in flat:
        if not any(x is z for z in arrays):
            arrays.append(x)
    where = [next(i for i, z in enumerate(arrays) if z is x) for x, _ in flat]
    n, rows, width = arrays[0].shape[-3:]
    olds = [] if into is None else list(into)
    order = [i * CHIPS + d for d in (0, 1, 3, 2) for i in range(CORES)]

    def kernel(*refs):
        ins = refs[: len(arrays)]
        outs = refs[len(arrays) + len(olds) + len(after) : -4]
        held, arrive, leave = refs[-3:]
        y, c = position()
        into_vmem, out_of = [], []
        for i in order:
            core = 1 - c if i >= CHIPS else c
            col = column(chip(y, -(i % CHIPS)), core, k)
            src = ins[where[i]]
            if flat[i][1] is not None:
                src = src.at[flat[i][1]]
            into_vmem.append(pltpu.make_async_copy(src, held.at[i], arrive.at[i]))
            out_of.append([
                pltpu.make_async_copy(
                    held.at[i, a], outs[a].at[:, pl.ds(col, width)], leave.at[i * n + a]
                )
                for a in range(n)
            ])
        run_two_stages(into_vmem, out_of)

    *outs, token = pl.pallas_call(
        kernel,
        out_shape=[jax.ShapeDtypeStruct((rows, PEERS * CHUNKS * WIDTH), jnp.bfloat16)] * n
        + [TOKEN],
        in_specs=[ANY] * (len(arrays) + len(olds) + len(after)),
        out_specs=[ANY] * (n + 1),
        scratch_shapes=[
            pltpu.VMEM((PEERS, n, rows, width), jnp.bfloat16),
            pltpu.SemaphoreType.DMA((PEERS,)),
            pltpu.SemaphoreType.DMA((PEERS * n,)),
        ],
        compiler_params=pltpu.CompilerParams(vmem_limit_bytes=VMEM),
        input_output_aliases={len(arrays) + a: a for a in range(len(olds))},
        cost_estimate=cost(0.05),
    )(*arrays, *olds, *after)
    return outs, [token]


def pick(parts, sender, after):
    groups = parts[0].shape[0]
    n = len(parts)

    def kernel(sender_ref, *refs):
        ins, out, (held, arrive, leave) = refs[:n], refs[n + len(after)], refs[-3:]
        into_vmem, out_of = [], []
        for g in range(groups):
            for k in range(n):
                i = g * n + k
                into_vmem.append(
                    pltpu.make_async_copy(ins[k].at[sender_ref[g]], held.at[i], arrive.at[i])
                )
                out_of.append([pltpu.make_async_copy(held.at[i], out.at[g, k], leave.at[i])])
        run_two_stages(into_vmem, out_of)

    slots, token = pl.pallas_call(
        kernel,
        out_shape=[jax.ShapeDtypeStruct((groups, n) + parts[0].shape[1:], jnp.bfloat16), TOKEN],
        grid_spec=pltpu.PrefetchScalarGridSpec(
            num_scalar_prefetch=1,
            grid=(1,),
            in_specs=[ANY] * (n + len(after)),
            out_specs=[ANY, ANY],
            scratch_shapes=[
                pltpu.VMEM((groups * n,) + parts[0].shape[1:], jnp.bfloat16),
                pltpu.SemaphoreType.DMA((groups * n,)),
                pltpu.SemaphoreType.DMA((groups * n,)),
            ],
        ),
        compiler_params=pltpu.CompilerParams(vmem_limit_bytes=VMEM),
        cost_estimate=cost(0.05),
    )(sender, *parts, *after)
    return slots, [token]


def settle(landed, after):
    _, peers, chunks, small, lanes = landed.shape
    groups = 8
    heads = landed.shape[0] // groups
    x = landed.reshape(heads, groups, peers, chunks, small, lanes)
    half = groups // 2

    def kernel(x_ref, *refs):
        o_ref = refs[len(after)]
        for s in range(peers):
            for k in range(chunks):
                for h in range(heads):
                    chip_, core = divmod(s, CORES)
                    col = (((chip_ * chunks + k) * CORES + core) * heads + h) * lanes
                    o_ref[:, col : col + lanes] = x_ref[h, :, s, k].reshape(half * small, lanes)

    mixed, token = pl.pallas_call(
        kernel,
        out_shape=[
            jax.ShapeDtypeStruct((groups * small, peers * chunks * heads * lanes), jnp.bfloat16),
            TOKEN,
        ],
        grid=(2,),
        in_specs=[
            pl.BlockSpec((heads, half, peers, chunks, small, lanes), lambda i: (0, i, 0, 0, 0, 0))
        ]
        + [ANY] * len(after),
        out_specs=[
            pl.BlockSpec((half * small, peers * chunks * heads * lanes), lambda i: (i, 0)),
            ANY,
        ],
        compiler_params=pltpu.CompilerParams(vmem_limit_bytes=VMEM),
        cost_estimate=cost(0.05),
    )(x, *after)
    return mixed, [token]


def triangle(after):
    a = lax.broadcasted_iota(jnp.int32, (ROWS, ROWS), 0)
    b = lax.broadcasted_iota(jnp.int32, (ROWS, ROWS), 1)
    return jnp.where((a > b) if after else (a < b), 1.0, 0.0).astype(jnp.bfloat16)


def gather_rows(pieces, scratch, scalars_ref):
    y, c = scalars_ref[0], scalars_ref[1]
    for i, ref in enumerate(pieces):
        p = chip(y, -(i % CHIPS)) * CORES + (1 - c if i >= CHIPS else c)
        x = ref[...]
        scratch[:, pl.ds(p, 1)] = x.reshape((scratch.shape[0], 1) + scratch.shape[2:])


def rows_of(ref, a, first, count, h):
    x = ref[a, pl.ds(first // 128, count // 128), :, h * HEAD_DIM : (h + 1) * HEAD_DIM]
    return x.reshape(count, HEAD_DIM)


def forward_kernel(scalars_ref, *refs):
    pieces = refs[:PEERS]
    out_ref, w_ref, sig_ref, _, tri_ref, acc_ref, qkv_ref = refs[-7:]
    heads = range(HP)
    i = pl.program_id(0)
    r0 = pl.multiple_of(i * ROWS, ROWS)

    @pl.when(i == 0)
    def _():
        tri_ref[...] = triangle(True)
        gather_rows(pieces, qkv_ref, scalars_ref)

    row = lax.broadcasted_iota(jnp.int32, (ROWS, 1), 0) + r0
    start = jnp.zeros((ROWS, 1), jnp.int32)
    for d in range(DOCS):
        first = scalars_ref[FIRSTS + d]
        start = jnp.where(row >= first, jnp.maximum(start, first), start)
    q = [rows_of(qkv_ref, 0, r0, ROWS, h) for h in heads]
    acc_ref[...] = jnp.zeros_like(acc_ref)

    def body(j, rest):
        lo = pl.multiple_of(r0 - j * ROWS, ROWS)
        col = lax.broadcasted_iota(jnp.int32, (ROWS, ROWS), 1) + lo
        allowed = (col >= start) & (col < row)
        left = []
        for h in heads:
            k, v = rows_of(qkv_ref, 1, lo, ROWS, h), rows_of(qkv_ref, 2, lo, ROWS, h)
            t = lax.dot_general(q[h], k, NT, preferred_element_type=jnp.float32)
            t = jnp.where(allowed, t * (SCALE * LOG2E), -1e30)
            tail = jnp.log2(1.0 + jnp.exp2(-jnp.abs(t)))
            z = jnp.maximum(t, 0.0) + tail
            ls = jnp.minimum(t, 0.0) - tail
            after = jnp.dot(
                z.astype(jnp.bfloat16), tri_ref[...], preferred_element_type=jnp.float32
            ) + rest[h]
            left.append(after[:, :1] + z[:, :1])
            w = jnp.exp2(ls - after).astype(jnp.bfloat16)
            acc_ref[h] += jnp.dot(w, v, preferred_element_type=jnp.float32)
            w_ref[h, 0, j] = w
            sig_ref[h, 0, j] = jnp.exp2(ls).astype(jnp.bfloat16)
        return tuple(left)

    lax.fori_loop(0, scalars_ref[2 + i], body, (jnp.zeros((ROWS, 1), jnp.float32),) * HP)

    for h in heads:
        x = acc_ref[h].astype(jnp.bfloat16)
        for r in range(ROWS // 128):
            for g in range(8):
                at = r * 128 + g * 16
                out_ref[h * 8 + g, pl.ds(r0 // 128 + r, 1), 0] = x[at : at + 16].reshape(
                    1, 16, HEAD_DIM
                )


def backward_kernel(by_chip, scalars_ref, *refs):
    pieces, (w_ref, sig_ref) = refs[:PEERS], refs[PEERS : PEERS + 2]
    outs = refs[-7 - (CHIPS if by_chip else PEERS) : -7]
    tri_ref, qkv_ref, dq_ref, acc_ref, dk_acc, dv_acc = refs[-6:]
    heads = range(HP)
    block = pl.program_id(0)
    r0 = pl.multiple_of(block * ROWS, ROWS)

    @pl.when(block == 0)
    def _():
        tri_ref[...] = triangle(False)
        gather_rows(pieces, qkv_ref, scalars_ref)
        dk_acc[...] = jnp.zeros_like(dk_acc)
        dv_acc[...] = jnp.zeros_like(dv_acc)

    q = [rows_of(qkv_ref, 0, r0, ROWS, h) for h in heads]
    g = [rows_of(qkv_ref, 3, r0, ROWS, h) for h in heads]
    acc_ref[...] = jnp.zeros_like(acc_ref)
    chunks = scalars_ref[2 + block]

    def body(i, upto):
        j = chunks - 1 - i
        lo = pl.multiple_of(r0 - j * ROWS, ROWS)
        here = pl.ds(lo, ROWS)
        right = []
        for h in heads:
            k, v = rows_of(qkv_ref, 1, lo, ROWS, h), rows_of(qkv_ref, 2, lo, ROWS, h)
            w = w_ref[h, 0, j]
            dv_acc[h, here] += lax.dot_general(w, g[h], TN, preferred_element_type=jnp.float32)
            dw = lax.dot_general(g[h], v, NT, preferred_element_type=jnp.float32)
            a = w.astype(jnp.float32) * dw
            total = jnp.dot(
                a.astype(jnp.bfloat16), tri_ref[...], preferred_element_type=jnp.float32
            ) + (a + upto[h])
            right.append(total[:, ROWS - 1 :])
            ds = (a - sig_ref[h, 0, j].astype(jnp.float32) * total).astype(jnp.bfloat16)
            acc_ref[h] += jnp.dot(ds, k, preferred_element_type=jnp.float32)
            dk_acc[h, here] += lax.dot_general(ds, q[h], TN, preferred_element_type=jnp.float32)
        return tuple(right)

    lax.fori_loop(0, chunks, body, (jnp.zeros((ROWS, 1), jnp.float32),) * HP)
    for h in heads:
        dq_ref[h, pl.ds(r0, ROWS)] = (acc_ref[h] * SCALE).astype(jnp.bfloat16)

    @pl.when(pl.program_id(0) == BLOCKS - 1)
    def _():
        y, c = scalars_ref[0], scalars_ref[1]
        for i in range(PEERS):
            d, sib = i % CHIPS, i // CHIPS
            ref = outs[d].at[sib] if by_chip else outs[i]
            p = chip(y, d) * CORES + (1 - c if sib else c)
            at = pl.ds(pl.multiple_of(p * 128, 128), 128)
            for h in heads:
                cols = slice(h * HEAD_DIM, (h + 1) * HEAD_DIM)
                ref[0, :, cols] = dq_ref[h, at]
                ref[1, :, cols] = (dk_acc[h, at] * SCALE).astype(jnp.bfloat16)
                ref[2, :, cols] = dv_acc[h, at].astype(jnp.bfloat16)


def kept_spec():
    return pl.BlockSpec((HP, 1) + KEPT[1:], lambda i, u: (0, i, 0, 0, 0))


def whole(shape):
    return pl.BlockSpec(shape, lambda i, u: (0,) * len(shape))


def forward(pieces, scalars, shared, k, after):
    kept = jax.ShapeDtypeStruct((HP,) + KEPT, jnp.bfloat16)
    out = (HP * 8, PEERS, CHUNKS, 16, HEAD_DIM)
    out_spec = pl.BlockSpec((HP * 8, PEERS, 1, 16, HEAD_DIM), lambda i, u: (0, 0, k, 0, 0))
    olds = [] if shared is None else [shared]
    out, *saved, token = pl.pallas_call(
        forward_kernel,
        out_shape=[jax.ShapeDtypeStruct(out, jnp.bfloat16), kept, kept, TOKEN],
        grid_spec=pltpu.PrefetchScalarGridSpec(
            num_scalar_prefetch=1,
            grid=(BLOCKS,),
            in_specs=[spec for _, spec in pieces] + [ANY] * (len(olds) + len(after)),
            out_specs=[out_spec, kept_spec(), kept_spec(), ANY],
            scratch_shapes=[
                pltpu.VMEM((ROWS, ROWS), jnp.bfloat16),
                pltpu.VMEM((HP, ROWS, HEAD_DIM), jnp.float32),
                pltpu.VMEM((3, PEERS, 128, WIDTH), jnp.bfloat16),
            ],
        ),
        compiler_params=pltpu.CompilerParams(vmem_limit_bytes=VMEM),
        input_output_aliases={1 + PEERS: 0} if olds else {},
        cost_estimate=cost(10 if k else 0.05),
    )(scalars, *[x for x, _ in pieces], *olds, *after)
    return out, saved, [token]


def backward(pieces, saved, scalars, by_chip, after):
    count = PEERS * 128
    outs = [(CORES, 3, 128, WIDTH)] * CHIPS if by_chip else [(3, 128, WIDTH)] * PEERS
    *grads, token = pl.pallas_call(
        functools.partial(backward_kernel, by_chip),
        out_shape=[jax.ShapeDtypeStruct(x, jnp.bfloat16) for x in outs] + [TOKEN],
        grid_spec=pltpu.PrefetchScalarGridSpec(
            num_scalar_prefetch=1,
            grid=(BLOCKS,),
            in_specs=[spec for _, spec in pieces]
            + [kept_spec(), kept_spec()]
            + [ANY] * len(after),
            out_specs=[whole(x) for x in outs] + [ANY],
            scratch_shapes=[
                pltpu.VMEM((ROWS, ROWS), jnp.bfloat16),
                pltpu.VMEM((4, PEERS, 128, WIDTH), jnp.bfloat16),
                pltpu.VMEM((HP, count, HEAD_DIM), jnp.bfloat16),
                pltpu.VMEM((HP, ROWS, HEAD_DIM), jnp.float32),
                pltpu.VMEM((HP, count, HEAD_DIM), jnp.float32),
                pltpu.VMEM((HP, count, HEAD_DIM), jnp.float32),
            ],
        ),
        compiler_params=pltpu.CompilerParams(vmem_limit_bytes=VMEM),
        cost_estimate=cost(15),
    )(scalars, *[x for x, _ in pieces], *saved, *after)
    return grads, [token]


def at_slabs(x, index, first, count):
    shape = (1, count) + x.shape[2:]
    return x, pl.BlockSpec(shape, lambda i, u: (index, first // count, 0, 0))


def at_first(x, first, count):
    return x, pl.BlockSpec((count,) + x.shape[1:], lambda i, u: (first // count, 0, 0))


def document_scalars(lengths, count):
    firsts = jnp.cumsum(lengths) - lengths
    places = jnp.arange(0, count, ROWS, dtype=jnp.int32)
    start = jnp.max(jnp.where(firsts[None, :] <= places[:, None], firsts[None, :], 0), axis=1)
    chunks = jnp.clip(places // ROWS - start // ROWS + 1, 1, jnp.minimum(places // ROWS + 1, PARTS))
    return jnp.concatenate([chunks, firsts]).astype(jnp.int32)


def local(queries, keys, values, grad_mixed, doc_lengths, owner):
    rows, width = queries.shape
    group = lax.axis_index("dp")
    groups = lax.axis_size("dp")

    lengths = lax.dynamic_index_in_dim(doc_lengths, group, 0, keepdims=False)
    y, c = position()
    scalars = jnp.concatenate(
        [jnp.stack([y, c]).astype(jnp.int32), document_scalars(lengths, rows * PEERS)]
    )
    ids = jnp.arange(groups, dtype=jnp.int32)
    sender = jnp.sum(jnp.where(owner[None, :] == ids[:, None], ids[None, :], 0), axis=1)
    sender = jnp.clip(sender, 0, groups - 1)

    inputs = [queries, keys, values, grad_mixed]

    slabs = [(a, 1) for a in range(4)]
    parts, other, token = pack(inputs, 0, slabs, [])
    own, sib = turn_direct(parts)
    swapped = swap_cores(other)
    second, token = merge_columns(inputs, swapped, slabs, token)
    second = turn_all(second)

    def chunk0(count):
        by_d = [at_first(x, 0, count) for x in own + sib[1:]]
        return by_d[:CHIPS] + [at_slabs(swapped, CHIPS, 0, count)] + by_d[CHIPS:]

    pieces = chunk0(3)
    out, saved, token = forward(pieces, scalars, None, 0, token)
    pieces = chunk0(4)
    got, token = backward(pieces, saved, scalars, True, token)
    got = turn_all(got)

    pieces = [at_slabs(x, core, 0, 3) for core in range(CORES) for x in second]
    out, saved, token = forward(pieces, scalars, out, 1, token)
    spread = lax.all_to_all(
        out.reshape(groups * PEERS * CHUNKS, 16, HEAD_DIM),
        ("dp", "seq"), split_axis=0, concat_axis=0, tiled=True,
    )
    pieces = [at_slabs(x, core, 0, 4) for core in range(CORES) for x in second]
    parts, token = backward(pieces, saved, scalars, False, token)
    parts = gate(parts, token + got[1:])
    own, sib = turn_direct(parts)

    (other,), token = pick_other_core_rows(got, sib[0], token)
    other = swap_cores(other)
    slots, token = pick([spread.reshape(groups, PEERS * CHUNKS, 16, HEAD_DIM)], sender, token)
    landed = lax.all_to_all(slots, "dp", split_axis=0, concat_axis=0, tiled=True)
    landed = landed.reshape(groups, PEERS, CHUNKS, 16, HEAD_DIM)

    near = [own[1], sib[1], own[3], sib[3]]
    grads, token = unpack(
        [(x, 0) for x in got], [(other, d) for d in range(CHIPS)], None, 0, token + near
    )
    grads, token = unpack(
        [(x, None) for x in own], [(other, CHIPS)] + [(x, None) for x in sib[1:]], grads, 1, token
    )
    mixed, token = settle(landed, token)
    return (mixed, grads[0], grads[1], grads[2])


def solution(mesh):
    placed = P(("dp", "seq"), None)
    return jax.shard_map(
        local,
        mesh=mesh,
        in_specs=(placed,) * 4 + (P(), P()),
        out_specs=(placed,) * 4,
        check_vma=False,
    )
```

```python
import functools

import jax
import jax.numpy as jnp
from jax import lax
from jax.experimental import pallas as pl
from jax.experimental.pallas import tpu as pltpu
from jax.sharding import PartitionSpec as P

HEAD_DIM = 128
LOG2E = 1.4426950408889634
SCALE = HEAD_DIM ** (-0.5)
ROWS = 256
CHIPS, CORES = 4, 2
PEERS = CHIPS * CORES
CHUNKS = 2
HP = 2
WIDTH = HP * HEAD_DIM
BLOCKS = PEERS * 128 // ROWS
DOCS = 8
FIRSTS = 2 + BLOCKS
PARTS = 3
KEPT = (BLOCKS, PARTS, ROWS, ROWS)
NT = (((1,), (1,)), ((), ()))
TN = (((0,), (0,)), ((), ()))
ANY = pl.BlockSpec(memory_space=pl.ANY)
MIB = 1024 * 1024
VMEM = 62 * MIB


def position():
    me = lax.axis_index("seq")
    return lax.div(me, CORES), lax.rem(me, CORES)


def chip(y, d):
    return lax.rem(y + d + CHIPS, CHIPS)


def column(y, c, k):
    return pl.multiple_of((y * CHUNKS + k) * CORES * WIDTH + c * WIDTH, WIDTH)


def turn(x, d):
    pairs = [(i, (i // CORES + d) % CHIPS * CORES + i % CORES) for i in range(PEERS)]
    return lax.ppermute(x, "seq", pairs)


def swap_cores(x):
    return lax.ppermute(x, "seq", [(i, i ^ 1) for i in range(PEERS)])


def turn_across(x, d):
    pairs = [(i, (i // CORES + d) % CHIPS * CORES + 1 - i % CORES) for i in range(PEERS)]
    return lax.ppermute(x, "seq", pairs)


def turn_direct(parts):
    own, sib = list(parts[:CHIPS]), list(parts[CHIPS:])
    for d in (1, 3, 2):
        own[d], sib[d] = turn(own[d], d), turn_across(sib[d], d)
    return own, sib


def turn_all(xs):
    got = {d: turn(xs[d], d) for d in (1, 3, 2)}
    return [xs[0], got[1], got[2], got[3]]


TOKEN = jax.ShapeDtypeStruct((8, 128), jnp.float32)


def cost(microseconds):
    return pl.CostEstimate(
        flops=int(microseconds * 1.1e9), bytes_accessed=MIB // 16, transcendentals=0
    )


def run_two_stages(into_vmem, out_of):
    for x in into_vmem:
        x.start()
    for x, nexts in zip(into_vmem, out_of):
        x.wait()
        for z in nexts:
            z.start()
    for nexts in out_of:
        for z in nexts:
            z.wait()


def copy_kernel(plan, inputs, shapes, pieces, after):
    n, m = len(inputs), len(pieces)

    def kernel(*refs):
        pairs = plan(refs[:n], refs[n + len(after) : -3 - m])
        held, arrive, leave = refs[-2 - m : -2], refs[-2], refs[-1]
        assert len(pairs) == m
        run_two_stages(
            [pltpu.make_async_copy(a, held[i], arrive.at[i]) for i, (a, _) in enumerate(pairs)],
            [[pltpu.make_async_copy(held[i], b, leave.at[i])] for i, (_, b) in enumerate(pairs)],
        )

    *outs, token = pl.pallas_call(
        kernel,
        out_shape=[jax.ShapeDtypeStruct(x, jnp.bfloat16) for x in shapes] + [TOKEN],
        in_specs=[ANY] * (n + len(after)),
        out_specs=[ANY] * (len(shapes) + 1),
        scratch_shapes=[pltpu.VMEM(x, jnp.bfloat16) for x in pieces]
        + [pltpu.SemaphoreType.DMA((m,)), pltpu.SemaphoreType.DMA((m,))],
        compiler_params=pltpu.CompilerParams(vmem_limit_bytes=VMEM),
        cost_estimate=cost(0.05),
    )(*inputs, *after)
    return outs, [token]


def gate(xs, after):
    def kernel(*refs):
        pass

    return pl.pallas_call(
        kernel,
        out_shape=[jax.ShapeDtypeStruct(x.shape, x.dtype) for x in xs],
        in_specs=[ANY] * (len(xs) + len(after)),
        out_specs=[ANY] * len(xs),
        input_output_aliases={i: i for i in range(len(xs))},
        compiler_params=pltpu.CompilerParams(vmem_limit_bytes=VMEM),
        cost_estimate=cost(0.05),
    )(*xs, *after)


def pack(arrays, k, slabs, after):
    n, rows = len(arrays), arrays[0].shape[0]
    parts = [(d, sib) for d in (1, 3, 2, 0) for sib in range(CORES) if (d, sib) != (0, 1)]

    def plan(ins, outs):
        y, c = position()
        return [
            (
                ins[a].at[:, pl.ds(column(chip(y, d), 1 - c if sib else c, k), WIDTH)],
                outs[i].at[a],
            )
            for i, (d, sib) in enumerate(parts)
            for a in range(n)
        ] + [
            (ins[a].at[:, pl.ds(column(chip(y, d), 1 - c, j), WIDTH)], outs[-1].at[o, i])
            for o, d in enumerate(list(range(CHIPS)) + [0])
            for i, (a, j) in enumerate(slabs if o < CHIPS else [(a, k) for a, _ in slabs])
        ]

    shapes = [(n, rows, WIDTH)] * len(parts) + [(CHIPS + 1, len(slabs), rows, WIDTH)]
    pieces = [(rows, WIDTH)] * (len(parts) * n + (CHIPS + 1) * len(slabs))
    (*outs, other), token = copy_kernel(plan, arrays, shapes, pieces, after)
    by_part = dict(zip(parts, outs))
    own = [by_part[d, 0] for d in range(CHIPS)]
    return own + [None] + [by_part[d, 1] for d in (1, 2, 3)], other, token


def merge_columns(arrays, swapped, slabs, after):
    rows, n = arrays[0].shape[0], len(slabs)

    def plan(ins, outs):
        y, c = position()
        pairs = []
        for d in (1, 3, 2, 0):
            for i, (a, k) in enumerate(slabs):
                src = ins[a].at[:, pl.ds(column(chip(y, d), c, k), WIDTH)]
                pairs.append((src, outs[d].at[0, i]))
            pairs.append((ins[-1].at[d], outs[d].at[1]))
        return pairs

    shapes = [(CORES, n, rows, WIDTH)] * CHIPS
    pieces = ([(rows, WIDTH)] * n + [(n, rows, WIDTH)]) * CHIPS
    return copy_kernel(plan, list(arrays) + [swapped], shapes, pieces, after)


def pick_other_core_rows(got, last, after):
    def plan(ins, outs):
        return [(ins[d].at[1], outs[0].at[d]) for d in range(CHIPS)] + [(ins[-1], outs[0].at[CHIPS])]

    shape = got[0].shape[1:]
    inputs = list(got) + [last]
    return copy_kernel(plan, inputs, [(CHIPS + 1,) + shape], [shape] * (CHIPS + 1), after)


def unpack(own, sib, into, k, turns, after):
    flat = [x[d] for d in turns for x in (own, sib)]
    arrays = []
    for x, _ in flat:
        if not any(x is z for z in arrays):
            arrays.append(x)
    where = [next(i for i, z in enumerate(arrays) if z is x) for x, _ in flat]
    n, rows, width = arrays[0].shape[-3:]
    olds = [] if into is None else list(into)

    def kernel(*refs):
        ins = refs[: len(arrays)]
        outs = refs[len(arrays) + len(olds) + len(after) : -4]
        held, arrive, leave = refs[-3:]
        y, c = position()
        into_vmem, out_of = [], []
        for i in range(len(flat)):
            col = column(chip(y, -turns[i // CORES]), 1 - c if i % CORES else c, k)
            src = ins[where[i]]
            if flat[i][1] is not None:
                src = src.at[flat[i][1]]
            into_vmem.append(pltpu.make_async_copy(src, held.at[i], arrive.at[i]))
            out_of.append([
                pltpu.make_async_copy(
                    held.at[i, a], outs[a].at[:, pl.ds(col, width)], leave.at[i * n + a]
                )
                for a in range(n)
            ])
        run_two_stages(into_vmem, out_of)

    *outs, token = pl.pallas_call(
        kernel,
        out_shape=[jax.ShapeDtypeStruct((rows, PEERS * CHUNKS * WIDTH), jnp.bfloat16)] * n
        + [TOKEN],
        in_specs=[ANY] * (len(arrays) + len(olds) + len(after)),
        out_specs=[ANY] * (n + 1),
        scratch_shapes=[
            pltpu.VMEM((len(flat), n, rows, width), jnp.bfloat16),
            pltpu.SemaphoreType.DMA((len(flat),)),
            pltpu.SemaphoreType.DMA((len(flat) * n,)),
        ],
        compiler_params=pltpu.CompilerParams(vmem_limit_bytes=VMEM),
        input_output_aliases={len(arrays) + a: a for a in range(len(olds))},
        cost_estimate=cost(0.05),
    )(*arrays, *olds, *after)
    return outs, [token]


def pick(parts, sender, after):
    groups = parts[0].shape[0]
    n = len(parts)

    def kernel(sender_ref, *refs):
        ins, out, (held, arrive, leave) = refs[:n], refs[n + len(after)], refs[-3:]
        into_vmem, out_of = [], []
        for g in range(groups):
            for k in range(n):
                i = g * n + k
                into_vmem.append(
                    pltpu.make_async_copy(ins[k].at[sender_ref[g]], held.at[i], arrive.at[i])
                )
                out_of.append([pltpu.make_async_copy(held.at[i], out.at[g, k], leave.at[i])])
        run_two_stages(into_vmem, out_of)

    slots, token = pl.pallas_call(
        kernel,
        out_shape=[jax.ShapeDtypeStruct((groups, n) + parts[0].shape[1:], jnp.bfloat16), TOKEN],
        grid_spec=pltpu.PrefetchScalarGridSpec(
            num_scalar_prefetch=1,
            grid=(1,),
            in_specs=[ANY] * (n + len(after)),
            out_specs=[ANY, ANY],
            scratch_shapes=[
                pltpu.VMEM((groups * n,) + parts[0].shape[1:], jnp.bfloat16),
                pltpu.SemaphoreType.DMA((groups * n,)),
                pltpu.SemaphoreType.DMA((groups * n,)),
            ],
        ),
        compiler_params=pltpu.CompilerParams(vmem_limit_bytes=VMEM),
        cost_estimate=cost(0.05),
    )(sender, *parts, *after)
    return slots, [token]


def settle(landed, after):
    _, peers, chunks, small, lanes = landed.shape
    groups = 8
    heads = landed.shape[0] // groups
    x = landed.reshape(heads, groups, peers, chunks, small, lanes)
    half = groups // 2

    def kernel(x_ref, *refs):
        o_ref = refs[len(after)]
        for s in range(peers):
            for k in range(chunks):
                for h in range(heads):
                    chip_, core = divmod(s, CORES)
                    col = (((chip_ * chunks + k) * CORES + core) * heads + h) * lanes
                    o_ref[:, col : col + lanes] = x_ref[h, :, s, k].reshape(half * small, lanes)

    mixed, token = pl.pallas_call(
        kernel,
        out_shape=[
            jax.ShapeDtypeStruct((groups * small, peers * chunks * heads * lanes), jnp.bfloat16),
            TOKEN,
        ],
        grid=(2,),
        in_specs=[
            pl.BlockSpec((heads, half, peers, chunks, small, lanes), lambda i: (0, i, 0, 0, 0, 0))
        ]
        + [ANY] * len(after),
        out_specs=[
            pl.BlockSpec((half * small, peers * chunks * heads * lanes), lambda i: (i, 0)),
            ANY,
        ],
        compiler_params=pltpu.CompilerParams(vmem_limit_bytes=VMEM),
        cost_estimate=cost(0.05),
    )(x, *after)
    return mixed, [token]


def triangle(after):
    a = lax.broadcasted_iota(jnp.int32, (ROWS, ROWS), 0)
    b = lax.broadcasted_iota(jnp.int32, (ROWS, ROWS), 1)
    return jnp.where((a > b) if after else (a < b), 1.0, 0.0).astype(jnp.bfloat16)


def gather_rows(pieces, scratch, scalars_ref):
    y, c = scalars_ref[0], scalars_ref[1]
    for i, ref in enumerate(pieces):
        p = chip(y, -(i % CHIPS)) * CORES + (1 - c if i >= CHIPS else c)
        x = ref[...]
        scratch[:, pl.ds(p, 1)] = x.reshape((scratch.shape[0], 1) + scratch.shape[2:])


def rows_of(ref, a, first, count, h):
    x = ref[a, pl.ds(first // 128, count // 128), :, h * HEAD_DIM : (h + 1) * HEAD_DIM]
    return x.reshape(count, HEAD_DIM)


def forward_kernel(scalars_ref, *refs):
    pieces = refs[:PEERS]
    out_ref, w_ref, sig_ref, _, tri_ref, acc_ref, qkv_ref = refs[-7:]
    heads = range(HP)
    i = pl.program_id(0)
    r0 = pl.multiple_of(i * ROWS, ROWS)

    @pl.when(i == 0)
    def _():
        tri_ref[...] = triangle(True)
        gather_rows(pieces, qkv_ref, scalars_ref)

    row = lax.broadcasted_iota(jnp.int32, (ROWS, 1), 0) + r0
    start = jnp.zeros((ROWS, 1), jnp.int32)
    for d in range(DOCS):
        first = scalars_ref[FIRSTS + d]
        start = jnp.where(row >= first, jnp.maximum(start, first), start)
    q = [rows_of(qkv_ref, 0, r0, ROWS, h) for h in heads]
    acc_ref[...] = jnp.zeros_like(acc_ref)

    def body(j, rest):
        lo = pl.multiple_of(r0 - j * ROWS, ROWS)
        col = lax.broadcasted_iota(jnp.int32, (ROWS, ROWS), 1) + lo
        allowed = (col >= start) & (col < row)
        left = []
        for h in heads:
            k, v = rows_of(qkv_ref, 1, lo, ROWS, h), rows_of(qkv_ref, 2, lo, ROWS, h)
            t = lax.dot_general(q[h], k, NT, preferred_element_type=jnp.float32)
            t = jnp.where(allowed, t * (SCALE * LOG2E), -1e30)
            tail = jnp.log2(1.0 + jnp.exp2(-jnp.abs(t)))
            z = jnp.maximum(t, 0.0) + tail
            ls = jnp.minimum(t, 0.0) - tail
            after = jnp.dot(
                z.astype(jnp.bfloat16), tri_ref[...], preferred_element_type=jnp.float32
            ) + rest[h]
            left.append(after[:, :1] + z[:, :1])
            w = jnp.exp2(ls - after).astype(jnp.bfloat16)
            acc_ref[h] += jnp.dot(w, v, preferred_element_type=jnp.float32)
            w_ref[h, 0, j] = w
            sig_ref[h, 0, j] = jnp.exp2(ls).astype(jnp.bfloat16)
        return tuple(left)

    lax.fori_loop(0, scalars_ref[2 + i], body, (jnp.zeros((ROWS, 1), jnp.float32),) * HP)

    for h in heads:
        x = acc_ref[h].astype(jnp.bfloat16)
        for r in range(ROWS // 128):
            for g in range(8):
                at = r * 128 + g * 16
                out_ref[h * 8 + g, pl.ds(r0 // 128 + r, 1), 0] = x[at : at + 16].reshape(
                    1, 16, HEAD_DIM
                )


def backward_kernel(by_chip, scalars_ref, *refs):
    pieces, (w_ref, sig_ref) = refs[:PEERS], refs[PEERS : PEERS + 2]
    outs = refs[-7 - (CHIPS if by_chip else PEERS) : -7]
    tri_ref, qkv_ref, dq_ref, acc_ref, dk_acc, dv_acc = refs[-6:]
    heads = range(HP)
    block = pl.program_id(0)
    r0 = pl.multiple_of(block * ROWS, ROWS)

    @pl.when(block == 0)
    def _():
        tri_ref[...] = triangle(False)
        gather_rows(pieces, qkv_ref, scalars_ref)
        dk_acc[...] = jnp.zeros_like(dk_acc)
        dv_acc[...] = jnp.zeros_like(dv_acc)

    q = [rows_of(qkv_ref, 0, r0, ROWS, h) for h in heads]
    g = [rows_of(qkv_ref, 3, r0, ROWS, h) for h in heads]
    acc_ref[...] = jnp.zeros_like(acc_ref)
    chunks = scalars_ref[2 + block]

    def body(i, upto):
        j = chunks - 1 - i
        lo = pl.multiple_of(r0 - j * ROWS, ROWS)
        here = pl.ds(lo, ROWS)
        right = []
        for h in heads:
            k, v = rows_of(qkv_ref, 1, lo, ROWS, h), rows_of(qkv_ref, 2, lo, ROWS, h)
            w = w_ref[h, 0, j]
            dv_acc[h, here] += lax.dot_general(w, g[h], TN, preferred_element_type=jnp.float32)
            dw = lax.dot_general(g[h], v, NT, preferred_element_type=jnp.float32)
            a = w.astype(jnp.float32) * dw
            total = jnp.dot(
                a.astype(jnp.bfloat16), tri_ref[...], preferred_element_type=jnp.float32
            ) + (a + upto[h])
            right.append(total[:, ROWS - 1 :])
            ds = (a - sig_ref[h, 0, j].astype(jnp.float32) * total).astype(jnp.bfloat16)
            acc_ref[h] += jnp.dot(ds, k, preferred_element_type=jnp.float32)
            dk_acc[h, here] += lax.dot_general(ds, q[h], TN, preferred_element_type=jnp.float32)
        return tuple(right)

    lax.fori_loop(0, chunks, body, (jnp.zeros((ROWS, 1), jnp.float32),) * HP)
    for h in heads:
        dq_ref[h, pl.ds(r0, ROWS)] = (acc_ref[h] * SCALE).astype(jnp.bfloat16)

    @pl.when(pl.program_id(0) == BLOCKS - 1)
    def _():
        y, c = scalars_ref[0], scalars_ref[1]
        for i in range(PEERS):
            d, sib = i % CHIPS, i // CHIPS
            ref = outs[d].at[sib] if by_chip else outs[i]
            p = chip(y, d) * CORES + (1 - c if sib else c)
            at = pl.ds(pl.multiple_of(p * 128, 128), 128)
            for h in heads:
                cols = slice(h * HEAD_DIM, (h + 1) * HEAD_DIM)
                ref[0, :, cols] = dq_ref[h, at]
                ref[1, :, cols] = (dk_acc[h, at] * SCALE).astype(jnp.bfloat16)
                ref[2, :, cols] = dv_acc[h, at].astype(jnp.bfloat16)


def kept_spec():
    return pl.BlockSpec((HP, 1) + KEPT[1:], lambda i, u: (0, i, 0, 0, 0))


def whole(shape):
    return pl.BlockSpec(shape, lambda i, u: (0,) * len(shape))


def forward(pieces, scalars, shared, k, after):
    kept = jax.ShapeDtypeStruct((HP,) + KEPT, jnp.bfloat16)
    out = (HP * 8, PEERS, CHUNKS, 16, HEAD_DIM)
    out_spec = pl.BlockSpec((HP * 8, PEERS, 1, 16, HEAD_DIM), lambda i, u: (0, 0, k, 0, 0))
    olds = [] if shared is None else [shared]
    out, *saved, token = pl.pallas_call(
        forward_kernel,
        out_shape=[jax.ShapeDtypeStruct(out, jnp.bfloat16), kept, kept, TOKEN],
        grid_spec=pltpu.PrefetchScalarGridSpec(
            num_scalar_prefetch=1,
            grid=(BLOCKS,),
            in_specs=[spec for _, spec in pieces] + [ANY] * (len(olds) + len(after)),
            out_specs=[out_spec, kept_spec(), kept_spec(), ANY],
            scratch_shapes=[
                pltpu.VMEM((ROWS, ROWS), jnp.bfloat16),
                pltpu.VMEM((HP, ROWS, HEAD_DIM), jnp.float32),
                pltpu.VMEM((3, PEERS, 128, WIDTH), jnp.bfloat16),
            ],
        ),
        compiler_params=pltpu.CompilerParams(vmem_limit_bytes=VMEM),
        input_output_aliases={1 + PEERS: 0} if olds else {},
        cost_estimate=cost(10 if k else 0.05),
    )(scalars, *[x for x, _ in pieces], *olds, *after)
    return out, saved, [token]


def backward(pieces, saved, scalars, by_chip, after):
    count = PEERS * 128
    outs = [(CORES, 3, 128, WIDTH)] * CHIPS if by_chip else [(3, 128, WIDTH)] * PEERS
    *grads, token = pl.pallas_call(
        functools.partial(backward_kernel, by_chip),
        out_shape=[jax.ShapeDtypeStruct(x, jnp.bfloat16) for x in outs] + [TOKEN],
        grid_spec=pltpu.PrefetchScalarGridSpec(
            num_scalar_prefetch=1,
            grid=(BLOCKS,),
            in_specs=[spec for _, spec in pieces]
            + [kept_spec(), kept_spec()]
            + [ANY] * len(after),
            out_specs=[whole(x) for x in outs] + [ANY],
            scratch_shapes=[
                pltpu.VMEM((ROWS, ROWS), jnp.bfloat16),
                pltpu.VMEM((4, PEERS, 128, WIDTH), jnp.bfloat16),
                pltpu.VMEM((HP, count, HEAD_DIM), jnp.bfloat16),
                pltpu.VMEM((HP, ROWS, HEAD_DIM), jnp.float32),
                pltpu.VMEM((HP, count, HEAD_DIM), jnp.float32),
                pltpu.VMEM((HP, count, HEAD_DIM), jnp.float32),
            ],
        ),
        compiler_params=pltpu.CompilerParams(vmem_limit_bytes=VMEM),
        cost_estimate=cost(15),
    )(scalars, *[x for x, _ in pieces], *saved, *after)
    return grads, [token]


def at_slabs(x, index, first, count):
    shape = (1, count) + x.shape[2:]
    return x, pl.BlockSpec(shape, lambda i, u: (index, first // count, 0, 0))


def at_first(x, first, count):
    return x, pl.BlockSpec((count,) + x.shape[1:], lambda i, u: (first // count, 0, 0))


def document_scalars(lengths, count):
    firsts = jnp.cumsum(lengths) - lengths
    places = jnp.arange(0, count, ROWS, dtype=jnp.int32)
    start = jnp.max(jnp.where(firsts[None, :] <= places[:, None], firsts[None, :], 0), axis=1)
    chunks = jnp.clip(places // ROWS - start // ROWS + 1, 1, jnp.minimum(places // ROWS + 1, PARTS))
    return jnp.concatenate([chunks, firsts]).astype(jnp.int32)


def local(queries, keys, values, grad_mixed, doc_lengths, owner):
    rows, width = queries.shape
    group = lax.axis_index("dp")
    groups = lax.axis_size("dp")

    lengths = lax.dynamic_index_in_dim(doc_lengths, group, 0, keepdims=False)
    y, c = position()
    scalars = jnp.concatenate(
        [jnp.stack([y, c]).astype(jnp.int32), document_scalars(lengths, rows * PEERS)]
    )
    ids = jnp.arange(groups, dtype=jnp.int32)
    sender = jnp.sum(jnp.where(owner[None, :] == ids[:, None], ids[None, :], 0), axis=1)
    sender = jnp.clip(sender, 0, groups - 1)

    inputs = [queries, keys, values, grad_mixed]

    slabs = [(a, 1) for a in range(4)]
    parts, other, token = pack(inputs, 0, slabs, [])
    own, sib = turn_direct(parts)
    swapped = swap_cores(other)
    second, token = merge_columns(inputs, swapped, slabs, token)
    second = turn_all(second)

    def chunk0(count):
        by_d = [at_first(x, 0, count) for x in own + sib[1:]]
        return by_d[:CHIPS] + [at_slabs(swapped, CHIPS, 0, count)] + by_d[CHIPS:]

    pieces = chunk0(3)
    out, saved, token = forward(pieces, scalars, None, 0, token)
    pieces = chunk0(4)
    got, token = backward(pieces, saved, scalars, True, token)
    got = turn_all(got)

    pieces = [at_slabs(x, core, 0, 3) for core in range(CORES) for x in second]
    out, saved, token = forward(pieces, scalars, out, 1, token)
    spread = lax.all_to_all(
        out.reshape(groups * PEERS * CHUNKS, 16, HEAD_DIM),
        ("dp", "seq"), split_axis=0, concat_axis=0, tiled=True,
    )
    pieces = [at_slabs(x, core, 0, 4) for core in range(CORES) for x in second]
    parts, token = backward(pieces, saved, scalars, False, token)
    parts = gate(parts, token + got[1:])
    own, sib = turn_direct(parts)

    (other,), token = pick_other_core_rows(got, sib[0], token)
    other = swap_cores(other)
    slots, token = pick([spread.reshape(groups, PEERS * CHUNKS, 16, HEAD_DIM)], sender, token)
    landed = lax.all_to_all(slots, "dp", split_axis=0, concat_axis=0, tiled=True)
    landed = landed.reshape(groups, PEERS, CHUNKS, 16, HEAD_DIM)

    near = [own[1], sib[1], own[3], sib[3]]
    grads, token = unpack(
        [(x, 0) for x in got], [(other, d) for d in range(CHIPS)], None, 0, (0, 1, 3, 2),
        token + near,
    )
    own = [(x, None) for x in own]
    sib = [(other, CHIPS)] + [(x, None) for x in sib[1:]]
    grads, token = unpack(own, sib, grads, 1, (0, 1, 3), token)
    mixed, token = settle(landed, token)
    grads, token = unpack(own, sib, grads, 1, (2,), token)
    return (mixed, grads[0], grads[1], grads[2])


def solution(mesh):
    placed = P(("dp", "seq"), None)
    return jax.shard_map(
        local,
        mesh=mesh,
        in_specs=(placed,) * 4 + (P(), P()),
        out_specs=(placed,) * 4,
        check_vma=False,
    )
```

```python
import functools

import jax
import jax.numpy as jnp
from jax import lax
from jax.experimental import pallas as pl
from jax.experimental.pallas import tpu as pltpu
from jax.sharding import PartitionSpec as P

HEAD_DIM = 128
LOG2E = 1.4426950408889634
SCALE = HEAD_DIM ** (-0.5)
ROWS = 256
CHIPS, CORES = 4, 2
PEERS = CHIPS * CORES
CHUNKS = 2
HP = 2
WIDTH = HP * HEAD_DIM
BLOCKS = PEERS * 128 // ROWS
DOCS = 8
FIRSTS = 2 + BLOCKS
PARTS = 3
KEPT = (BLOCKS, PARTS, ROWS, ROWS)
NT = (((1,), (1,)), ((), ()))
TN = (((0,), (0,)), ((), ()))
ANY = pl.BlockSpec(memory_space=pl.ANY)
MIB = 1024 * 1024
VMEM = 62 * MIB


def position():
    me = lax.axis_index("seq")
    return lax.div(me, CORES), lax.rem(me, CORES)


def chip(y, d):
    return lax.rem(y + d + CHIPS, CHIPS)


def column(y, c, k):
    return pl.multiple_of((y * CHUNKS + k) * CORES * WIDTH + c * WIDTH, WIDTH)


def turn(x, d):
    pairs = [(i, (i // CORES + d) % CHIPS * CORES + i % CORES) for i in range(PEERS)]
    return lax.ppermute(x, "seq", pairs)


def swap_cores(x):
    return lax.ppermute(x, "seq", [(i, i ^ 1) for i in range(PEERS)])


def turn_across(x, d):
    pairs = [(i, (i // CORES + d) % CHIPS * CORES + 1 - i % CORES) for i in range(PEERS)]
    return lax.ppermute(x, "seq", pairs)


def turn_direct(parts):
    own, sib = list(parts[:CHIPS]), list(parts[CHIPS:])
    for d in (1, 3, 2):
        own[d], sib[d] = turn(own[d], d), turn_across(sib[d], d)
    return own, sib


def turn_all(xs):
    got = {d: turn(xs[d], d) for d in (1, 3, 2)}
    return [xs[0], got[1], got[2], got[3]]


TOKEN = jax.ShapeDtypeStruct((8, 128), jnp.float32)


def cost(microseconds):
    return pl.CostEstimate(
        flops=int(microseconds * 1.1e9), bytes_accessed=MIB // 16, transcendentals=0
    )


def run_two_stages(into_vmem, out_of):
    for x in into_vmem:
        x.start()
    for x, nexts in zip(into_vmem, out_of):
        x.wait()
        for z in nexts:
            z.start()
    for nexts in out_of:
        for z in nexts:
            z.wait()


def copy_kernel(plan, inputs, shapes, pieces, after):
    n, m = len(inputs), len(pieces)

    def kernel(*refs):
        pairs = plan(refs[:n], refs[n + len(after) : -3 - m])
        held, arrive, leave = refs[-2 - m : -2], refs[-2], refs[-1]
        assert len(pairs) == m
        run_two_stages(
            [pltpu.make_async_copy(a, held[i], arrive.at[i]) for i, (a, _) in enumerate(pairs)],
            [[pltpu.make_async_copy(held[i], b, leave.at[i])] for i, (_, b) in enumerate(pairs)],
        )

    *outs, token = pl.pallas_call(
        kernel,
        out_shape=[jax.ShapeDtypeStruct(x, jnp.bfloat16) for x in shapes] + [TOKEN],
        in_specs=[ANY] * (n + len(after)),
        out_specs=[ANY] * (len(shapes) + 1),
        scratch_shapes=[pltpu.VMEM(x, jnp.bfloat16) for x in pieces]
        + [pltpu.SemaphoreType.DMA((m,)), pltpu.SemaphoreType.DMA((m,))],
        compiler_params=pltpu.CompilerParams(vmem_limit_bytes=VMEM),
        cost_estimate=cost(0.05),
    )(*inputs, *after)
    return outs, [token]


def gate(xs, after):
    def kernel(*refs):
        pass

    return pl.pallas_call(
        kernel,
        out_shape=[jax.ShapeDtypeStruct(x.shape, x.dtype) for x in xs],
        in_specs=[ANY] * (len(xs) + len(after)),
        out_specs=[ANY] * len(xs),
        input_output_aliases={i: i for i in range(len(xs))},
        compiler_params=pltpu.CompilerParams(vmem_limit_bytes=VMEM),
        cost_estimate=cost(0.05),
    )(*xs, *after)


def pack(arrays, k, slabs, after):
    n, rows = len(arrays), arrays[0].shape[0]
    parts = [(d, sib) for d in (1, 3, 2, 0) for sib in range(CORES) if (d, sib) != (0, 1)]

    def plan(ins, outs):
        y, c = position()
        return [
            (
                ins[a].at[:, pl.ds(column(chip(y, d), 1 - c if sib else c, k), WIDTH)],
                outs[i].at[a],
            )
            for i, (d, sib) in enumerate(parts)
            for a in range(n)
        ] + [
            (ins[a].at[:, pl.ds(column(chip(y, d), 1 - c, j), WIDTH)], outs[-1].at[o, i])
            for o, d in enumerate(list(range(CHIPS)) + [0])
            for i, (a, j) in enumerate(slabs if o < CHIPS else [(a, k) for a, _ in slabs])
        ]

    shapes = [(n, rows, WIDTH)] * len(parts) + [(CHIPS + 1, len(slabs), rows, WIDTH)]
    pieces = [(rows, WIDTH)] * (len(parts) * n + (CHIPS + 1) * len(slabs))
    (*outs, other), token = copy_kernel(plan, arrays, shapes, pieces, after)
    by_part = dict(zip(parts, outs))
    own = [by_part[d, 0] for d in range(CHIPS)]
    return own + [None] + [by_part[d, 1] for d in (1, 2, 3)], other, token


def merge_columns(arrays, swapped, slabs, after):
    rows, n = arrays[0].shape[0], len(slabs)

    def plan(ins, outs):
        y, c = position()
        pairs = []
        for d in (1, 3, 2, 0):
            for i, (a, k) in enumerate(slabs):
                src = ins[a].at[:, pl.ds(column(chip(y, d), c, k), WIDTH)]
                pairs.append((src, outs[d].at[0, i]))
            pairs.append((ins[-1].at[d], outs[d].at[1]))
        return pairs

    shapes = [(CORES, n, rows, WIDTH)] * CHIPS
    pieces = ([(rows, WIDTH)] * n + [(n, rows, WIDTH)]) * CHIPS
    return copy_kernel(plan, list(arrays) + [swapped], shapes, pieces, after)


def pick_other_core_rows(got, last, after):
    def plan(ins, outs):
        return [(ins[d].at[1], outs[0].at[d]) for d in range(CHIPS)] + [(ins[-1], outs[0].at[CHIPS])]

    shape = got[0].shape[1:]
    inputs = list(got) + [last]
    return copy_kernel(plan, inputs, [(CHIPS + 1,) + shape], [shape] * (CHIPS + 1), after)


def unpack(own, sib, into, k, after):
    flat = list(own) + list(sib)
    arrays = []
    for x, _ in flat:
        if not any(x is z for z in arrays):
            arrays.append(x)
    where = [next(i for i, z in enumerate(arrays) if z is x) for x, _ in flat]
    n, rows, width = arrays[0].shape[-3:]
    olds = [] if into is None else list(into)
    order = [i * CHIPS + d for d in (0, 1, 3, 2) for i in range(CORES)]

    def kernel(*refs):
        ins = refs[: len(arrays)]
        outs = refs[len(arrays) + len(olds) + len(after) : -4]
        held, arrive, leave = refs[-3:]
        y, c = position()
        into_vmem, out_of = [], []
        for i in order:
            core = 1 - c if i >= CHIPS else c
            col = column(chip(y, -(i % CHIPS)), core, k)
            src = ins[where[i]]
            if flat[i][1] is not None:
                src = src.at[flat[i][1]]
            into_vmem.append(pltpu.make_async_copy(src, held.at[i], arrive.at[i]))
            out_of.append([
                pltpu.make_async_copy(
                    held.at[i, a], outs[a].at[:, pl.ds(col, width)], leave.at[i * n + a]
                )
                for a in range(n)
            ])
        run_two_stages(into_vmem, out_of)

    *outs, token = pl.pallas_call(
        kernel,
        out_shape=[jax.ShapeDtypeStruct((rows, PEERS * CHUNKS * WIDTH), jnp.bfloat16)] * n
        + [TOKEN],
        in_specs=[ANY] * (len(arrays) + len(olds) + len(after)),
        out_specs=[ANY] * (n + 1),
        scratch_shapes=[
            pltpu.VMEM((PEERS, n, rows, width), jnp.bfloat16),
            pltpu.SemaphoreType.DMA((PEERS,)),
            pltpu.SemaphoreType.DMA((PEERS * n,)),
        ],
        compiler_params=pltpu.CompilerParams(vmem_limit_bytes=VMEM),
        input_output_aliases={len(arrays) + a: a for a in range(len(olds))},
        cost_estimate=cost(0.05),
    )(*arrays, *olds, *after)
    return outs, [token]


def pick(parts, sender, after):
    groups = parts[0].shape[0]
    n = len(parts)

    def kernel(sender_ref, *refs):
        ins, out, (held, arrive, leave) = refs[:n], refs[n + len(after)], refs[-3:]
        into_vmem, out_of = [], []
        for g in range(groups):
            for k in range(n):
                i = g * n + k
                into_vmem.append(
                    pltpu.make_async_copy(ins[k].at[sender_ref[g]], held.at[i], arrive.at[i])
                )
                out_of.append([pltpu.make_async_copy(held.at[i], out.at[g, k], leave.at[i])])
        run_two_stages(into_vmem, out_of)

    slots, token = pl.pallas_call(
        kernel,
        out_shape=[jax.ShapeDtypeStruct((groups, n) + parts[0].shape[1:], jnp.bfloat16), TOKEN],
        grid_spec=pltpu.PrefetchScalarGridSpec(
            num_scalar_prefetch=1,
            grid=(1,),
            in_specs=[ANY] * (n + len(after)),
            out_specs=[ANY, ANY],
            scratch_shapes=[
                pltpu.VMEM((groups * n,) + parts[0].shape[1:], jnp.bfloat16),
                pltpu.SemaphoreType.DMA((groups * n,)),
                pltpu.SemaphoreType.DMA((groups * n,)),
            ],
        ),
        compiler_params=pltpu.CompilerParams(vmem_limit_bytes=VMEM),
        cost_estimate=cost(0.05),
    )(sender, *parts, *after)
    return slots, [token]


def settle(landed, after):
    _, peers, chunks, small, lanes = landed.shape
    groups = 8
    heads = landed.shape[0] // groups
    x = landed.reshape(heads, groups, peers, chunks, small, lanes)
    half = groups // 2

    def kernel(x_ref, *refs):
        o_ref = refs[len(after)]
        for s in range(peers):
            for k in range(chunks):
                for h in range(heads):
                    chip_, core = divmod(s, CORES)
                    col = (((chip_ * chunks + k) * CORES + core) * heads + h) * lanes
                    o_ref[:, col : col + lanes] = x_ref[h, :, s, k].reshape(half * small, lanes)

    mixed, token = pl.pallas_call(
        kernel,
        out_shape=[
            jax.ShapeDtypeStruct((groups * small, peers * chunks * heads * lanes), jnp.bfloat16),
            TOKEN,
        ],
        grid=(2,),
        in_specs=[
            pl.BlockSpec((heads, half, peers, chunks, small, lanes), lambda i: (0, i, 0, 0, 0, 0))
        ]
        + [ANY] * len(after),
        out_specs=[
            pl.BlockSpec((half * small, peers * chunks * heads * lanes), lambda i: (i, 0)),
            ANY,
        ],
        compiler_params=pltpu.CompilerParams(vmem_limit_bytes=VMEM),
        cost_estimate=cost(0.05),
    )(x, *after)
    return mixed, [token]


def triangle(after):
    a = lax.broadcasted_iota(jnp.int32, (ROWS, ROWS), 0)
    b = lax.broadcasted_iota(jnp.int32, (ROWS, ROWS), 1)
    return jnp.where((a > b) if after else (a < b), 1.0, 0.0).astype(jnp.bfloat16)


def gather_rows(pieces, scratch, scalars_ref):
    y, c = scalars_ref[0], scalars_ref[1]
    for i, ref in enumerate(pieces):
        p = chip(y, -(i % CHIPS)) * CORES + (1 - c if i >= CHIPS else c)
        x = ref[...]
        scratch[:, pl.ds(p, 1)] = x.reshape((scratch.shape[0], 1) + scratch.shape[2:])


def rows_of(ref, a, first, count, h):
    x = ref[a, pl.ds(first // 128, count // 128), :, h * HEAD_DIM : (h + 1) * HEAD_DIM]
    return x.reshape(count, HEAD_DIM)


def forward_kernel(scalars_ref, *refs):
    pieces = refs[:PEERS]
    out_ref, w_ref, sig_ref, _, tri_ref, acc_ref, qkv_ref = refs[-7:]
    heads = range(HP)
    i = pl.program_id(0)
    r0 = pl.multiple_of(i * ROWS, ROWS)

    @pl.when(i == 0)
    def _():
        tri_ref[...] = triangle(True)
        gather_rows(pieces, qkv_ref, scalars_ref)

    row = lax.broadcasted_iota(jnp.int32, (ROWS, 1), 0) + r0
    start = jnp.zeros((ROWS, 1), jnp.int32)
    for d in range(DOCS):
        first = scalars_ref[FIRSTS + d]
        start = jnp.where(row >= first, jnp.maximum(start, first), start)
    q = [rows_of(qkv_ref, 0, r0, ROWS, h) for h in heads]
    acc_ref[...] = jnp.zeros_like(acc_ref)

    def body(j, rest):
        lo = pl.multiple_of(r0 - j * ROWS, ROWS)
        col = lax.broadcasted_iota(jnp.int32, (ROWS, ROWS), 1) + lo
        allowed = (col >= start) & (col < row)
        left = []
        for h in heads:
            k, v = rows_of(qkv_ref, 1, lo, ROWS, h), rows_of(qkv_ref, 2, lo, ROWS, h)
            t = lax.dot_general(q[h], k, NT, preferred_element_type=jnp.float32)
            t = jnp.where(allowed, t * (SCALE * LOG2E), -1e30)
            tail = jnp.log2(1.0 + jnp.exp2(-jnp.abs(t)))
            z = jnp.maximum(t, 0.0) + tail
            ls = jnp.minimum(t, 0.0) - tail
            after = jnp.dot(
                z.astype(jnp.bfloat16), tri_ref[...], preferred_element_type=jnp.float32
            ) + rest[h]
            left.append(after[:, :1] + z[:, :1])
            w = jnp.exp2(ls - after).astype(jnp.bfloat16)
            acc_ref[h] += jnp.dot(w, v, preferred_element_type=jnp.float32)
            w_ref[h, 0, j] = w
            sig_ref[h, 0, j] = jnp.exp2(ls).astype(jnp.bfloat16)
        return tuple(left)

    lax.fori_loop(0, scalars_ref[2 + i], body, (jnp.zeros((ROWS, 1), jnp.float32),) * HP)

    for h in heads:
        x = acc_ref[h].astype(jnp.bfloat16)
        for r in range(ROWS // 128):
            for g in range(8):
                at = r * 128 + g * 16
                out_ref[h * 8 + g, pl.ds(r0 // 128 + r, 1), 0] = x[at : at + 16].reshape(
                    1, 16, HEAD_DIM
                )


def backward_kernel(by_chip, scalars_ref, *refs):
    pieces, (w_ref, sig_ref) = refs[:PEERS], refs[PEERS : PEERS + 2]
    outs = refs[-7 - (CHIPS if by_chip else PEERS) : -7]
    tri_ref, qkv_ref, dq_ref, acc_ref, dk_acc, dv_acc = refs[-6:]
    heads = range(HP)
    block = pl.program_id(0)
    r0 = pl.multiple_of(block * ROWS, ROWS)

    @pl.when(block == 0)
    def _():
        tri_ref[...] = triangle(False)
        gather_rows(pieces, qkv_ref, scalars_ref)
        dk_acc[...] = jnp.zeros_like(dk_acc)
        dv_acc[...] = jnp.zeros_like(dv_acc)

    q = [rows_of(qkv_ref, 0, r0, ROWS, h) for h in heads]
    g = [rows_of(qkv_ref, 3, r0, ROWS, h) for h in heads]
    acc_ref[...] = jnp.zeros_like(acc_ref)
    chunks = scalars_ref[2 + block]

    def body(i, upto):
        j = chunks - 1 - i
        lo = pl.multiple_of(r0 - j * ROWS, ROWS)
        here = pl.ds(lo, ROWS)
        right = []
        for h in heads:
            k, v = rows_of(qkv_ref, 1, lo, ROWS, h), rows_of(qkv_ref, 2, lo, ROWS, h)
            w = w_ref[h, 0, j]
            dv_acc[h, here] += lax.dot_general(w, g[h], TN, preferred_element_type=jnp.float32)
            dw = lax.dot_general(g[h], v, NT, preferred_element_type=jnp.float32)
            a = w.astype(jnp.float32) * dw
            total = jnp.dot(
                a.astype(jnp.bfloat16), tri_ref[...], preferred_element_type=jnp.float32
            ) + (a + upto[h])
            right.append(total[:, ROWS - 1 :])
            ds = (a - sig_ref[h, 0, j].astype(jnp.float32) * total).astype(jnp.bfloat16)
            acc_ref[h] += jnp.dot(ds, k, preferred_element_type=jnp.float32)
            dk_acc[h, here] += lax.dot_general(ds, q[h], TN, preferred_element_type=jnp.float32)
        return tuple(right)

    lax.fori_loop(0, chunks, body, (jnp.zeros((ROWS, 1), jnp.float32),) * HP)
    for h in heads:
        dq_ref[h, pl.ds(r0, ROWS)] = (acc_ref[h] * SCALE).astype(jnp.bfloat16)

    @pl.when(pl.program_id(0) == BLOCKS - 1)
    def _():
        y, c = scalars_ref[0], scalars_ref[1]
        for i in range(PEERS):
            d, sib = i % CHIPS, i // CHIPS
            ref = outs[d].at[sib] if by_chip else outs[i]
            p = chip(y, d) * CORES + (1 - c if sib else c)
            at = pl.ds(pl.multiple_of(p * 128, 128), 128)
            for h in heads:
                cols = slice(h * HEAD_DIM, (h + 1) * HEAD_DIM)
                ref[0, :, cols] = dq_ref[h, at]
                ref[1, :, cols] = (dk_acc[h, at] * SCALE).astype(jnp.bfloat16)
                ref[2, :, cols] = dv_acc[h, at].astype(jnp.bfloat16)


def kept_spec():
    return pl.BlockSpec((HP, 1) + KEPT[1:], lambda i, u: (0, i, 0, 0, 0))


def whole(shape):
    return pl.BlockSpec(shape, lambda i, u: (0,) * len(shape))


def forward(pieces, scalars, shared, k, after):
    kept = jax.ShapeDtypeStruct((HP,) + KEPT, jnp.bfloat16)
    out = (HP * 8, PEERS, CHUNKS, 16, HEAD_DIM)
    out_spec = pl.BlockSpec((HP * 8, PEERS, 1, 16, HEAD_DIM), lambda i, u: (0, 0, k, 0, 0))
    olds = [] if shared is None else [shared]
    out, *saved, token = pl.pallas_call(
        forward_kernel,
        out_shape=[jax.ShapeDtypeStruct(out, jnp.bfloat16), kept, kept, TOKEN],
        grid_spec=pltpu.PrefetchScalarGridSpec(
            num_scalar_prefetch=1,
            grid=(BLOCKS,),
            in_specs=[spec for _, spec in pieces] + [ANY] * (len(olds) + len(after)),
            out_specs=[out_spec, kept_spec(), kept_spec(), ANY],
            scratch_shapes=[
                pltpu.VMEM((ROWS, ROWS), jnp.bfloat16),
                pltpu.VMEM((HP, ROWS, HEAD_DIM), jnp.float32),
                pltpu.VMEM((3, PEERS, 128, WIDTH), jnp.bfloat16),
            ],
        ),
        compiler_params=pltpu.CompilerParams(vmem_limit_bytes=VMEM),
        input_output_aliases={1 + PEERS: 0} if olds else {},
        cost_estimate=cost(10 if k else 0.05),
    )(scalars, *[x for x, _ in pieces], *olds, *after)
    return out, saved, [token]


def backward(pieces, saved, scalars, by_chip, after):
    count = PEERS * 128
    outs = [(CORES, 3, 128, WIDTH)] * CHIPS if by_chip else [(3, 128, WIDTH)] * PEERS
    *grads, token = pl.pallas_call(
        functools.partial(backward_kernel, by_chip),
        out_shape=[jax.ShapeDtypeStruct(x, jnp.bfloat16) for x in outs] + [TOKEN],
        grid_spec=pltpu.PrefetchScalarGridSpec(
            num_scalar_prefetch=1,
            grid=(BLOCKS,),
            in_specs=[spec for _, spec in pieces]
            + [kept_spec(), kept_spec()]
            + [ANY] * len(after),
            out_specs=[whole(x) for x in outs] + [ANY],
            scratch_shapes=[
                pltpu.VMEM((ROWS, ROWS), jnp.bfloat16),
                pltpu.VMEM((4, PEERS, 128, WIDTH), jnp.bfloat16),
                pltpu.VMEM((HP, count, HEAD_DIM), jnp.bfloat16),
                pltpu.VMEM((HP, ROWS, HEAD_DIM), jnp.float32),
                pltpu.VMEM((HP, count, HEAD_DIM), jnp.float32),
                pltpu.VMEM((HP, count, HEAD_DIM), jnp.float32),
            ],
        ),
        compiler_params=pltpu.CompilerParams(vmem_limit_bytes=VMEM),
        cost_estimate=cost(15),
    )(scalars, *[x for x, _ in pieces], *saved, *after)
    return grads, [token]


def at_slabs(x, index, first, count):
    shape = (1, count) + x.shape[2:]
    return x, pl.BlockSpec(shape, lambda i, u: (index, first // count, 0, 0))


def at_first(x, first, count):
    return x, pl.BlockSpec((count,) + x.shape[1:], lambda i, u: (first // count, 0, 0))


def document_scalars(lengths, count):
    firsts = jnp.cumsum(lengths) - lengths
    places = jnp.arange(0, count, ROWS, dtype=jnp.int32)
    start = jnp.max(jnp.where(firsts[None, :] <= places[:, None], firsts[None, :], 0), axis=1)
    chunks = jnp.clip(places // ROWS - start // ROWS + 1, 1, jnp.minimum(places // ROWS + 1, PARTS))
    return jnp.concatenate([chunks, firsts]).astype(jnp.int32)


def local(queries, keys, values, grad_mixed, doc_lengths, owner):
    rows, width = queries.shape
    group = lax.axis_index("dp")
    groups = lax.axis_size("dp")

    lengths = lax.dynamic_index_in_dim(doc_lengths, group, 0, keepdims=False)
    y, c = position()
    scalars = jnp.concatenate(
        [jnp.stack([y, c]).astype(jnp.int32), document_scalars(lengths, rows * PEERS)]
    )
    ids = jnp.arange(groups, dtype=jnp.int32)
    sender = jnp.sum(jnp.where(owner[None, :] == ids[:, None], ids[None, :], 0), axis=1)
    sender = jnp.clip(sender, 0, groups - 1)

    inputs = [queries, keys, values, grad_mixed]

    slabs = [(a, 1) for a in range(4)]
    parts, other, token = pack(inputs, 0, slabs, [])
    own, sib = turn_direct(parts)
    swapped = swap_cores(other)
    second, token = merge_columns(inputs, swapped, slabs, token)
    second = turn_all(second)

    def chunk0(count):
        by_d = [at_first(x, 0, count) for x in own + sib[1:]]
        return by_d[:CHIPS] + [at_slabs(swapped, CHIPS, 0, count)] + by_d[CHIPS:]

    pieces = chunk0(3)
    out, saved, token = forward(pieces, scalars, None, 0, token)
    pieces = chunk0(4)
    got, token = backward(pieces, saved, scalars, True, token)
    got = turn_all(got)

    pieces = [at_slabs(x, core, 0, 3) for core in range(CORES) for x in second]
    out, saved, token = forward(pieces, scalars, out, 1, token)
    spread = lax.all_to_all(
        out.reshape(groups * PEERS * CHUNKS, 16, HEAD_DIM),
        ("dp", "seq"), split_axis=0, concat_axis=0, tiled=True,
    )
    pieces = [at_slabs(x, core, 0, 4) for core in range(CORES) for x in second]
    parts, token = backward(pieces, saved, scalars, False, token)
    parts = gate(parts, token + got[1:])
    own, sib = turn_direct(parts)

    (other,), token = pick_other_core_rows(got, sib[0], token)
    other = swap_cores(other)
    slots, token = pick([spread.reshape(groups, PEERS * CHUNKS, 16, HEAD_DIM)], sender, token)
    landed = lax.all_to_all(slots, "dp", split_axis=0, concat_axis=0, tiled=True)
    landed = landed.reshape(groups, PEERS, CHUNKS, 16, HEAD_DIM)

    grads, token = unpack(
        [(x, 0) for x in got], [(other, d) for d in range(CHIPS)], None, 0, token
    )
    grads, token = unpack(
        [(x, None) for x in own], [(other, CHIPS)] + [(x, None) for x in sib[1:]], grads, 1, token
    )
    mixed, token = settle(landed, token)
    return (mixed, grads[0], grads[1], grads[2])


def solution(mesh):
    placed = P(("dp", "seq"), None)
    return jax.shard_map(
        local,
        mesh=mesh,
        in_specs=(placed,) * 4 + (P(), P()),
        out_specs=(placed,) * 4,
        check_vma=False,
    )
```
